256 devices in a mesh: attn: 32 (over z, x), tensor: 8 (over y, core).
Axes of the slice: x: 4, y: 4, z: 8, core: 2. Of those that a mesh axis runs over, the one named last changes fastest.
Arguments:
- queries: bfloat16 [32, 8192], P('attn', 'tensor'), may hold values from -4.5 to 4.5
- fresh_keys: bfloat16 [32, 1024], P('attn', 'tensor'), may hold values from -10 to 10
- fresh_values: bfloat16 [32, 1024], P('attn', 'tensor'), may hold values from -6 to 6
- key_cache_blocks: bfloat16 [1024, 512, 1024], P('attn', None, 'tensor'), may hold values from -100 to 100
- value_cache_blocks: bfloat16 [1024, 512, 1024], P('attn', None, 'tensor'), may hold values from -6 to 6
- lengths: int32 [32], replicated, may hold values from 2 to 127488, as said below
- placement: int32 [32, 249], replicated, may hold values from -1 to 1023, as said below
- w_out: bfloat16 [8192, 8192], P('tensor', 'attn'), may hold values from -0.0625 to 0.0625
Outputs:
- projected: bfloat16 [32, 8192], P(None, ('attn', 'tensor'))
The draws below stay inside these ranges and needn't reach their ends.
Inputs may be any that keep to these rules, and one draw needn't show every extreme that they name: A row's cache takes ceil(lengths / 512) blocks, at most 249; all rows together take at most 1024 blocks. `placement`: entry j of row r names the block (index along attn times 32 plus slot) holding the row's tokens j * 512 to (j + 1) * 512 - 1 for j < ceil(lengths[r] / 512), and is -1 beyond; no block is named twice.
All inputs are finite; a program needn't handle non-finite values.
Results may differ from the reference program's by a relative error of at most 0.0075.
Values may be sent and summed in bfloat16 or wider, within the bound.
No kernel may reach another device: no remote copies, remote signals or barrier semaphores. Data moves between devices by JAX's collectives and lax.ppermute only.
A program may use at most 64 MiB of HBM per device.

```python
import math
import jax
import jax.numpy as jnp
from jax import lax

D = 8192
QUERY_HEADS = 64
KEY_VALUE_HEADS = 8
HEAD_SIZE = 128
BLOCK_TOKENS = 512
SLOTS = 32
ROW_DEV = 1
DECODE_ROWS = 32
TOTAL_BLOCKS = 1024
MAXBLK = 249


def block_layout(key):
    key = jax.random.fold_in(key, 7001)
    key_draws, key_pick, key_rows, key_tail, key_slots = jax.random.split(key, 5)
    group_count = DECODE_ROWS // 8
    capacity = 8 * SLOTS // ROW_DEV
    fractions = jax.random.randint(key_draws, (group_count, 8), 0, 1 << 20)
    remaining = jnp.full((group_count,), capacity, jnp.int32)
    counts_list = []
    for member in range(8):
        room_left = remaining - (7 - member)
        taken = 1 + fractions[:, member] % room_left
        counts_list.append(taken)
        remaining = remaining - taken
    counts = jnp.stack(counts_list, axis=1)
    chosen = jax.random.randint(key_pick, (), 0, group_count)
    extreme = jnp.concatenate([jnp.full((1,), MAXBLK, jnp.int32), jnp.ones((7,), jnp.int32)])
    chosen_group = (jnp.arange(group_count) == chosen)[:, None]
    counts = jnp.where(chosen_group, extreme[None, :], counts)
    short_flag = jnp.logical_and(chosen_group, (jnp.arange(8) > 0)[None, :]).astype(jnp.int32)
    row_order = jax.random.permutation(key_rows, DECODE_ROWS)
    blocks_per_row = counts.reshape(DECODE_ROWS)[row_order]
    short_rows = short_flag.reshape(DECODE_ROWS)[row_order]
    tail_tokens = jax.random.randint(key_tail, (DECODE_ROWS,), 2, BLOCK_TOKENS + 1)
    tail_tokens = jnp.where(short_rows == 1, 2 + tail_tokens % 8, tail_tokens)
    row_lengths = jnp.where(blocks_per_row == MAXBLK, MAXBLK * BLOCK_TOKENS, (blocks_per_row - 1) * BLOCK_TOKENS + tail_tokens)
    starts_at = jnp.cumsum(blocks_per_row) - blocks_per_row
    order_slots = jax.random.permutation(key_slots, TOTAL_BLOCKS)
    head_slot = order_slots[0]
    order_slots = jnp.where(order_slots == TOTAL_BLOCKS - 1, head_slot, order_slots)
    order_slots = order_slots.at[0].set(TOTAL_BLOCKS - 1)
    position = jnp.arange(MAXBLK)
    flat_index = jnp.minimum(starts_at[:, None] + position[None, :], TOTAL_BLOCKS - 1)
    placed = jnp.where(position[None, :] < blocks_per_row[:, None], order_slots[flat_index], -1)
    return (row_lengths.astype(jnp.int32), placed.astype(jnp.int32))


def query_parts(key):
    key = jax.random.fold_in(key, 7002)
    noise_random_key = jax.random.fold_in(key, 1)
    jitter_term = jnp.clip(jax.random.normal(noise_random_key, (DECODE_ROWS, KEY_VALUE_HEADS, QUERY_HEADS // KEY_VALUE_HEADS, HEAD_SIZE), jnp.float32), -3.0, 3.0)
    return jitter_term


def draw_queries(key, part):
    jitter_term = query_parts(key)
    blended_draw = jitter_term
    return blended_draw.reshape(DECODE_ROWS, QUERY_HEADS * HEAD_SIZE).astype(jnp.bfloat16)


def draw_key_cache_blocks(key, part):
    key = jax.random.fold_in(key, 2)
    base_random_key = jax.random.fold_in(key, 0)
    base_draw = jnp.clip(jax.random.normal(base_random_key, (TOTAL_BLOCKS, BLOCK_TOKENS, KEY_VALUE_HEADS * HEAD_SIZE), jnp.float32), -4.0, 4.0)
    return base_draw.astype(jnp.bfloat16)


def draw_lengths(key, part):
    row_lengths, placed = block_layout(key)
    return row_lengths


def draw_placement(key, part):
    row_lengths, placed = block_layout(key)
    return placed


def block_scale(rng, shape, pieces, smallest, high):
    level, own = 1.0, jax.random.fold_in(rng, 6)
    for dim, blocks in pieces:
        draws = jnp.exp(jax.random.uniform(jax.random.fold_in(own, dim), (blocks,), jnp.float32, smallest / len(pieces), high / len(pieces)))
        level = level * jnp.repeat(draws, shape[dim] // blocks).reshape([-1 if axis == dim else 1 for axis in range(len(shape))])
    return level


def centred(own_key, shape, width, reach, cuts=(), kind=jnp.bfloat16):
    array = width * jax.random.normal(own_key, shape, jnp.float32)
    if cuts:
        array = array * block_scale(own_key, shape, cuts, -0.22, 0.18)
    return jnp.clip(array, -reach, reach).astype(kind)


def setup_inputs(seed: int = 0) -> dict:
    splits = jax.random.split(jax.random.key(seed), 9)
    return {
        "queries": draw_queries(jax.random.fold_in(splits[8], 71), 0),
        "fresh_keys": centred(splits[1], (DECODE_ROWS, KEY_VALUE_HEADS * HEAD_SIZE), 2.0, 10.0, ((0, 32), (1, 8))),
        "fresh_values": centred(splits[2], (DECODE_ROWS, KEY_VALUE_HEADS * HEAD_SIZE), 1.0, 6.0, ((0, 32), (1, 8))),
        "key_cache_blocks": draw_key_cache_blocks(jax.random.fold_in(splits[8], 71), 0),
        "value_cache_blocks": centred(splits[4], (TOTAL_BLOCKS, BLOCK_TOKENS, KEY_VALUE_HEADS * HEAD_SIZE), 1.0, 6.0, ((0, 32), (2, 8))),
        "lengths": draw_lengths(jax.random.fold_in(splits[8], 71), 0),
        "placement": draw_placement(jax.random.fold_in(splits[8], 71), 0),
        "w_out": centred(splits[7], (QUERY_HEADS * HEAD_SIZE, D), (QUERY_HEADS * HEAD_SIZE) ** -0.5, 0.0625, ((0, 8), (1, 32))),
    }


def reference(queries, fresh_keys, fresh_values, key_cache_blocks, value_cache_blocks, lengths, placement, w_out):
    group_width = QUERY_HEADS // KEY_VALUE_HEADS
    logit_scale = 1.0 / math.sqrt(HEAD_SIZE)
    spanned_tokens = MAXBLK * BLOCK_TOKENS

    def one_row(row_items):
        query_vector, single_key_row, single_value_row, row_length, row_places = row_items
        block_numbers = jnp.maximum(row_places, 0).astype(jnp.int32)
        keys_of_row = key_cache_blocks[block_numbers].reshape(spanned_tokens, KEY_VALUE_HEADS, HEAD_SIZE).astype(jnp.float32)
        values_of_row = value_cache_blocks[block_numbers].reshape(spanned_tokens, KEY_VALUE_HEADS, HEAD_SIZE).astype(jnp.float32)
        heads_of_row = query_vector.reshape(KEY_VALUE_HEADS, group_width, HEAD_SIZE).astype(jnp.float32)
        is_valid = jnp.arange(spanned_tokens, dtype=jnp.int32) < row_length
        scores = jnp.einsum('kgd,tkd->kgt', heads_of_row, keys_of_row) * logit_scale
        scores = jnp.where(is_valid, scores, -1e+30)
        self_score = jnp.einsum('izr,ir->iz', heads_of_row, single_key_row.reshape(KEY_VALUE_HEADS, HEAD_SIZE).astype(jnp.float32)) * logit_scale
        highest = jnp.maximum(lax.optimization_barrier(jnp.max(scores, axis=-1)), self_score)
        weights = jnp.where(is_valid, jnp.exp(scores - highest[..., None]), 0.0)
        own_weight = jnp.exp(self_score - highest)
        denominator = lax.optimization_barrier(jnp.sum(weights, axis=-1)) + own_weight
        rounded = lax.optimization_barrier(weights.astype(jnp.bfloat16)).astype(jnp.float32)
        self_rounded = lax.optimization_barrier(own_weight.astype(jnp.bfloat16)).astype(jnp.float32)
        blended_draw = jnp.einsum('kgt,tkd->kgd', rounded, values_of_row)
        blended_draw = blended_draw + self_rounded[..., None] * single_value_row.reshape(KEY_VALUE_HEADS, 1, HEAD_SIZE).astype(jnp.float32)
        return (blended_draw / denominator[..., None]).reshape(QUERY_HEADS * HEAD_SIZE).astype(jnp.bfloat16)
    attended = lax.map(one_row, (queries, fresh_keys, fresh_values, lengths, placement))
    return jnp.dot(attended, w_out, preferred_element_type=jnp.float32).astype(jnp.bfloat16)
```

```python
import math

import jax
import jax.numpy as jnp
from jax import lax
from jax.experimental import pallas as pl
from jax.experimental.pallas import tpu as pltpu
from jax.sharding import PartitionSpec as P

QUERY_HEADS = 64
KEY_VALUE_HEADS = 8
HEAD_SIZE = 128
GROUP = QUERY_HEADS // KEY_VALUE_HEADS
SCALE = 1.0 / math.sqrt(HEAD_SIZE)
LOW = -1e30
LIVE_BITS = 10

VMEM = pl.BlockSpec(memory_space=pltpu.VMEM)
SMEM = pl.BlockSpec(memory_space=pltpu.SMEM)


def slots_kernel(first_ref, lengths_ref, placement_ref, code_ref):
    places = placement_ref[...] - first_ref[0]
    row = lax.broadcasted_iota(jnp.int32, places.shape, 0)
    start = lax.broadcasted_iota(jnp.int32, places.shape, 1) * 512
    live = jnp.clip(lengths_ref[...] - start, 0, 512)
    code = row * (1 << LIVE_BITS) + live
    for slot in range(code_ref.shape[0]):
        code_ref[slot] = jnp.sum(jnp.where(places == slot, code, 0))


def attention_kernel(code_ref, query_ref, key_ref, value_ref, out_ref, scores, peaks, masses, sums):
    slots, block, _ = key_ref.shape
    rows = query_ref.shape[0]
    contract_last = (((1,), (1,)), ((), ()))
    position = lax.broadcasted_iota(jnp.int32, (GROUP, block), 1)
    peaks[...] = jnp.full_like(peaks, LOW)
    masses[...] = jnp.zeros_like(masses)
    sums[...] = jnp.zeros_like(sums)
    for slot in range(slots):
        code = code_ref[slot]
        row = code >> LIVE_BITS
        live = code & ((1 << LIVE_BITS) - 1)
        s = lax.dot_general(
            query_ref[row], key_ref[slot], contract_last, preferred_element_type=jnp.float32
        )
        s = jnp.where(position < live, s * SCALE, LOW)
        scores[slot] = s
        top = s[:, :128]
        for part in range(1, block // 128):
            top = jnp.maximum(top, s[:, part * 128 : (part + 1) * 128])
        peaks[row] = jnp.maximum(peaks[row], top)
    top = jnp.max(peaks[...], axis=-1, keepdims=True)
    top = top.astype(jnp.bfloat16).astype(jnp.float32)
    peaks[...] = jnp.broadcast_to(top, peaks.shape)
    for slot in range(slots):
        code = code_ref[slot]
        row = code >> LIVE_BITS
        live = code & ((1 << LIVE_BITS) - 1)
        w = jnp.exp(scores[slot] - jnp.tile(peaks[row], (1, block // 128)))
        w = jnp.where(position < live, w, 0.0)
        mass = w[:, :128]
        for part in range(1, block // 128):
            mass = mass + w[:, part * 128 : (part + 1) * 128]
        masses[row] = masses[row] + mass
        sums[row] = sums[row] + jnp.dot(
            w.astype(jnp.bfloat16), value_ref[slot], preferred_element_type=jnp.float32
        )
    mass = jnp.sum(masses[...], axis=-1, keepdims=True)
    high = mass.astype(jnp.bfloat16).astype(jnp.float32)
    lane = lax.broadcasted_iota(jnp.int32, (rows, GROUP, 128), 2)
    extra = jnp.where(lane == 0, peaks[...], jnp.where(lane == 1, high, mass - high))
    out_ref[...] = jnp.concatenate([sums[...], extra], axis=1).astype(jnp.bfloat16)


def finish_kernel(parts_ref, query_ref, key_ref, value_ref, out_ref):
    parts = parts_ref[...].astype(jnp.float32)
    partial = parts[:, :GROUP]
    extra = parts[:, GROUP:]
    own = jnp.sum(
        query_ref[0].astype(jnp.float32) * key_ref[...].astype(jnp.float32), axis=-1, keepdims=True
    )
    own = own * SCALE
    peaks = extra[:, :, 0:1]
    highest = jnp.maximum(jnp.max(peaks, axis=0), own)
    factor = jnp.exp(peaks - highest[None])
    own_weight = jnp.exp(own - highest)
    masses = extra[:, :, 1:2] + extra[:, :, 2:3]
    denominator = jnp.sum(masses * factor, axis=0) + own_weight
    total = jnp.sum(partial * factor, axis=0)
    total = total + own_weight.astype(jnp.bfloat16).astype(jnp.float32) * value_ref[...].astype(
        jnp.float32
    )
    attended = (total / denominator).astype(jnp.bfloat16)
    out_ref[...] = jnp.broadcast_to(attended[None], out_ref.shape)


def project_kernel(attended_ref, w_ref, out_ref):
    heads = jnp.swapaxes(attended_ref[...].astype(jnp.float32), 0, 1).astype(jnp.bfloat16)
    total = None
    for head in range(GROUP):
        term = jnp.dot(
            heads[head],
            w_ref[head * HEAD_SIZE : (head + 1) * HEAD_SIZE, :],
            preferred_element_type=jnp.float32,
        )
        total = term if total is None else total + term
    width = out_ref.shape[2]
    for part in range(out_ref.shape[0]):
        out_ref[part] = total[:, part * width : (part + 1) * width]


def shards(
    queries,
    fresh_keys,
    fresh_values,
    key_cache_blocks,
    value_cache_blocks,
    lengths,
    placement,
    w_out,
):
    rows = lengths.shape[0]
    slots = key_cache_blocks.shape[0]
    first = (lax.axis_index("attn") * slots).astype(jnp.int32).reshape(1)
    codes = pl.pallas_call(
        slots_kernel,
        out_shape=jax.ShapeDtypeStruct((slots,), jnp.int32),
        in_specs=[SMEM, VMEM, VMEM],
        out_specs=SMEM,
        name="slots",
    )(first, lengths.reshape(rows, 1), placement)

    own_query = queries.reshape(1, GROUP, HEAD_SIZE)
    every_query = lax.all_to_all(
        jnp.broadcast_to(own_query, (rows, GROUP, HEAD_SIZE)), "attn", 0, 0, tiled=True
    )
    state = pltpu.VMEM((rows, GROUP, 128), jnp.float32)
    partials = pl.pallas_call(
        attention_kernel,
        out_shape=jax.ShapeDtypeStruct((rows, 2 * GROUP, HEAD_SIZE), jnp.bfloat16),
        in_specs=[SMEM, VMEM, VMEM, VMEM],
        out_specs=VMEM,
        scratch_shapes=[pltpu.VMEM((slots, GROUP, key_cache_blocks.shape[1]), jnp.float32), state, state, state],
        name="attention",
    )(codes, every_query, key_cache_blocks, value_cache_blocks)
    partials = lax.all_to_all(partials, "attn", 0, 0, tiled=True)
    attended = pl.pallas_call(
        finish_kernel,
        out_shape=jax.ShapeDtypeStruct((rows, GROUP, HEAD_SIZE), jnp.bfloat16),
        in_specs=[VMEM] * 4,
        out_specs=VMEM,
        name="finish",
    )(partials, own_query, fresh_keys, fresh_values)
    attended = lax.all_to_all(attended, "attn", 0, 0, tiled=True)
    ranks = lax.axis_size("tensor")
    terms = pl.pallas_call(
        project_kernel,
        out_shape=jax.ShapeDtypeStruct((ranks, rows, w_out.shape[1] // ranks), jnp.float32),
        in_specs=[VMEM] * 2,
        out_specs=VMEM,
        name="project",
    )(attended, w_out)
    terms = lax.all_to_all(terms, "tensor", 0, 0, tiled=True)
    return jnp.sum(terms, axis=0).astype(jnp.bfloat16)


def solution(mesh):
    return jax.shard_map(
        shards,
        mesh=mesh,
        in_specs=(
            P("attn", "tensor"),
            P("attn", "tensor"),
            P("attn", "tensor"),
            P("attn", None, "tensor"),
            P("attn", None, "tensor"),
            P(),
            P(),
            P("tensor", "attn"),
        ),
        out_specs=P(None, ("attn", "tensor")),
        check_vma=False,
    )
```

```python
import math

import jax
import jax.numpy as jnp
from jax import lax
from jax.experimental import pallas as pl
from jax.experimental.pallas import tpu as pltpu
from jax.sharding import PartitionSpec as P

QUERY_HEADS = 64
KEY_VALUE_HEADS = 8
HEAD_SIZE = 128
BLOCK = 512
GROUP = QUERY_HEADS // KEY_VALUE_HEADS
SCALE = 1.0 / math.sqrt(HEAD_SIZE)
LOW = -1e30
LIVE_BITS = 10

VMEM = pl.BlockSpec(memory_space=pltpu.VMEM)
SMEM = pl.BlockSpec(memory_space=pltpu.SMEM)
ANY = pl.BlockSpec(memory_space=pl.ANY)
PIECES = 2


def load(*copies):
    for copy in copies:
        copy.start()
    for copy in copies:
        copy.wait()


def spread_kernel(query_hbm, key_hbm, value_hbm, out_ref, own_ref, query, key, value, sems):
    pairs = ((query_hbm, query), (key_hbm, key), (value_hbm, value))
    load(*(pltpu.make_async_copy(*pair, sems.at[i]) for i, pair in enumerate(pairs)))
    wide = query[...].astype(jnp.float32)
    heads = [wide[:, head * HEAD_SIZE : (head + 1) * HEAD_SIZE] for head in range(GROUP)]
    heads = jnp.concatenate(heads, axis=0)
    out_ref[...] = jnp.broadcast_to(heads.astype(jnp.bfloat16)[None], out_ref.shape)
    score = SCALE * jnp.sum(heads * key[...].astype(jnp.float32), axis=-1, keepdims=True)
    own_ref[0] = jnp.broadcast_to(score, (GROUP, HEAD_SIZE))
    own_ref[1] = jnp.broadcast_to(value[...].astype(jnp.float32), (GROUP, HEAD_SIZE))


def slots_kernel(device_ref, lengths_hbm, placement_hbm, code_ref, lengths, placement, sems):
    pairs = ((lengths_hbm, lengths), (placement_hbm, placement))
    load(*(pltpu.make_async_copy(*pair, sems.at[i]) for i, pair in enumerate(pairs)))
    slots = code_ref.shape[0]
    places = placement[...] - device_ref[0] * slots
    row = lax.broadcasted_iota(jnp.int32, places.shape, 0)
    length = jnp.zeros_like(places)
    for r in range(lengths_hbm.shape[0]):
        length = jnp.where(row == r, lengths[r], length)
    start = lax.broadcasted_iota(jnp.int32, places.shape, 1) * BLOCK
    code = (row << LIVE_BITS) + jnp.clip(length - start, 0, BLOCK)
    for slot in range(slots):
        code_ref[slot] = jnp.sum(jnp.where(places == slot, code, 0))


def attention_kernel(
    device_ref,
    code_ref,
    query_ref,
    own_ref,
    key_hbm,
    value_hbm,
    out_ref,
    keys,
    values,
    sems,
    scores,
    peaks,
    masses,
    sums,
):
    slots, block, _ = keys.shape
    rows = query_ref.shape[0]
    device = device_ref[0]
    per_piece = slots // PIECES
    copies = [
        [
            pltpu.make_async_copy(
                source.at[pl.ds(piece * per_piece, per_piece)],
                target.at[pl.ds(piece * per_piece, per_piece)],
                sems.at[which, piece],
            )
            for piece in range(PIECES)
        ]
        for which, (source, target) in enumerate(((key_hbm, keys), (value_hbm, values)))
    ]
    for copy in (*copies[0], *copies[1]):
        copy.start()

    contract_last = (((1,), (1,)), ((), ()))
    position = lax.broadcasted_iota(jnp.int32, (GROUP, block), 1)
    lane = lax.broadcasted_iota(jnp.int32, (rows, GROUP, 128), 2)
    masses[...] = jnp.zeros_like(masses)
    sums[...] = jnp.zeros_like(sums)
    peaks[...] = jnp.full_like(peaks, LOW)
    own_score = own_ref[0]
    peaks[device] = own_score

    held = []
    for slot in range(slots):
        code = code_ref[slot]
        held.append((code >> LIVE_BITS, code & ((1 << LIVE_BITS) - 1)))
    for slot, (row, live) in enumerate(held):
        if slot % per_piece == 0:
            copies[0][slot // per_piece].wait()
        s = lax.dot_general(
            query_ref[row], keys[slot], contract_last, preferred_element_type=jnp.float32
        )
        s = jnp.where(position < live, s * SCALE, LOW)
        scores[slot] = s
        top = s[:, :128]
        for part in range(1, block // 128):
            top = jnp.maximum(top, s[:, part * 128 : (part + 1) * 128])
        peaks[row] = jnp.maximum(peaks[row], top)
    top = jnp.max(peaks[...], axis=-1, keepdims=True)
    top = top.astype(jnp.bfloat16).astype(jnp.float32)
    peaks[...] = jnp.broadcast_to(top, peaks.shape)
    own_weight = jnp.exp(own_score - peaks[device])
    masses[device] = jnp.where(lane[0] == 0, own_weight, 0.0)
    sums[device] = own_weight.astype(jnp.bfloat16).astype(jnp.float32) * own_ref[1]
    for slot, (row, live) in enumerate(held):
        if slot % per_piece == 0:
            copies[1][slot // per_piece].wait()
        w = jnp.exp(scores[slot] - jnp.tile(peaks[row], (1, block // 128)))
        w = jnp.where(position < live, w, 0.0)
        mass = w[:, :128]
        for part in range(1, block // 128):
            mass = mass + w[:, part * 128 : (part + 1) * 128]
        masses[row] = masses[row] + mass
        sums[row] = sums[row] + jnp.dot(
            w.astype(jnp.bfloat16), values[slot], preferred_element_type=jnp.float32
        )
    mass = jnp.sum(masses[...], axis=-1, keepdims=True)
    high = mass.astype(jnp.bfloat16).astype(jnp.float32)
    extra = jnp.where(lane == 0, peaks[...], jnp.where(lane == 1, high, mass - high))
    out_ref[...] = jnp.concatenate([sums[...], extra], axis=1).astype(jnp.bfloat16)


def finish_kernel(parts_ref, out_ref):
    parts = parts_ref[...].astype(jnp.float32)
    partial = parts[:, :GROUP]
    extra = parts[:, GROUP:]
    peaks = extra[:, :, 0:1]
    highest = jnp.max(peaks, axis=0, keepdims=True)
    factor = jnp.exp(peaks - highest)
    masses = extra[:, :, 1:2] + extra[:, :, 2:3]
    denominator = jnp.sum(masses * factor, axis=0)
    total = jnp.sum(partial * factor, axis=0)
    attended = (total / denominator).astype(jnp.bfloat16)
    out_ref[...] = jnp.broadcast_to(attended[None], out_ref.shape)


def project_kernel(attended_ref, w_ref, out_ref):
    heads = jnp.swapaxes(attended_ref[...].astype(jnp.float32), 0, 1).astype(jnp.bfloat16)
    total = None
    for head in range(GROUP):
        term = jnp.dot(
            heads[head],
            w_ref[head * HEAD_SIZE : (head + 1) * HEAD_SIZE, :],
            preferred_element_type=jnp.float32,
        )
        total = term if total is None else total + term
    ranks, packed, full = out_ref.shape
    width = total.shape[1] // ranks
    for rank in range(ranks):
        block = total[:, rank * width : (rank + 1) * width]
        out_ref[rank] = jnp.concatenate(
            [block[i * packed : (i + 1) * packed] for i in range(full // width)], axis=1
        )


def sum_kernel(terms_ref, out_ref):
    total = jnp.sum(terms_ref[...], axis=0)
    width = out_ref.shape[1]
    out_ref[...] = jnp.concatenate(
        [total[:, i * width : (i + 1) * width] for i in range(total.shape[1] // width)], axis=0
    ).astype(jnp.bfloat16)


def in_hbm(x):
    return pltpu.with_memory_space_constraint(x, pltpu.HBM)


def call(kernel, name, out_shape, in_specs, scratch_shapes=(), megabytes=2):
    return pl.pallas_call(
        kernel,
        out_shape=out_shape,
        in_specs=in_specs,
        out_specs=jax.tree.map(lambda _: VMEM, out_shape),
        scratch_shapes=scratch_shapes,
        compiler_params=pltpu.CompilerParams(vmem_limit_bytes=megabytes << 20),
        name=name,
    )


def shards(
    queries,
    fresh_keys,
    fresh_values,
    key_cache_blocks,
    value_cache_blocks,
    lengths,
    placement,
    w_out,
):
    rows = lengths.shape[0]
    slots, block, _ = key_cache_blocks.shape
    device = lax.axis_index("attn").astype(jnp.int32).reshape(1)
    ranks = lax.axis_size("tensor")
    per_row = jax.ShapeDtypeStruct((rows, GROUP, HEAD_SIZE), jnp.bfloat16)

    fresh = (queries, fresh_keys, fresh_values)
    spread, own = call(
        spread_kernel,
        "spread",
        (per_row, jax.ShapeDtypeStruct((2, GROUP, HEAD_SIZE), jnp.float32)),
        [ANY] * 3,
        [pltpu.VMEM(a.shape, a.dtype) for a in fresh] + [pltpu.SemaphoreType.DMA((3,))],
    )(*map(in_hbm, fresh))
    every_query = lax.all_to_all(spread, "attn", 0, 0, tiled=True)
    codes = pl.pallas_call(
        slots_kernel,
        out_shape=jax.ShapeDtypeStruct((slots,), jnp.int32),
        in_specs=[SMEM, ANY, ANY],
        out_specs=SMEM,
        scratch_shapes=[
            pltpu.SMEM(lengths.shape, jnp.int32),
            pltpu.VMEM(placement.shape, jnp.int32),
            pltpu.SemaphoreType.DMA((2,)),
        ],
        compiler_params=pltpu.CompilerParams(vmem_limit_bytes=2 << 20),
        name="slots",
    )(device, in_hbm(lengths), in_hbm(placement))
    cache = pltpu.VMEM(key_cache_blocks.shape, jnp.bfloat16)
    state = pltpu.VMEM((rows, GROUP, 128), jnp.float32)
    partials = call(
        attention_kernel,
        "attention",
        jax.ShapeDtypeStruct((rows, 2 * GROUP, HEAD_SIZE), jnp.bfloat16),
        [SMEM, SMEM, VMEM, VMEM, ANY, ANY],
        [
            cache,
            cache,
            pltpu.SemaphoreType.DMA((2, PIECES)),
            pltpu.VMEM((slots, GROUP, block), jnp.float32),
            state,
            state,
            state,
        ],
        16,
    )(
        device,
        codes,
        every_query,
        own,
        in_hbm(key_cache_blocks),
        in_hbm(value_cache_blocks),
    )
    partials = lax.all_to_all(partials, "attn", 0, 0, tiled=True)
    attended = call(finish_kernel, "finish", per_row, [VMEM])(partials)
    attended = lax.all_to_all(attended, "attn", 0, 0, tiled=True)

    width = w_out.shape[1] // ranks
    terms = call(
        project_kernel,
        "project",
        jax.ShapeDtypeStruct((ranks, rows * width // 128, 128), jnp.float32),
        [VMEM, VMEM],
        (),
        4,
    )(attended, w_out)
    terms = lax.all_to_all(terms, "tensor", 0, 0, tiled=True)
    return call(sum_kernel, "sum", jax.ShapeDtypeStruct((rows, width), jnp.bfloat16), [VMEM])(terms)


def solution(mesh):
    return jax.shard_map(
        shards,
        mesh=mesh,
        in_specs=(
            P("attn", "tensor"),
            P("attn", "tensor"),
            P("attn", "tensor"),
            P("attn", None, "tensor"),
            P("attn", None, "tensor"),
            P(),
            P(),
            P("tensor", "attn"),
        ),
        out_specs=P(None, ("attn", "tensor")),
        check_vma=False,
    )
```

```python
import math

import jax
import jax.numpy as jnp
from jax import lax
from jax.experimental import pallas as pl
from jax.experimental.pallas import tpu as pltpu
from jax.sharding import PartitionSpec as P

QUERY_HEADS = 64
KEY_VALUE_HEADS = 8
HEAD_SIZE = 128
BLOCK = 512
GROUP = QUERY_HEADS // KEY_VALUE_HEADS
SCALE = 1.0 / math.sqrt(HEAD_SIZE)
LOW = -(2.0**99)
LIVE_BITS = 10

VMEM = pl.BlockSpec(memory_space=pltpu.VMEM)
SMEM = pl.BlockSpec(memory_space=pltpu.SMEM)
ANY = pl.BlockSpec(memory_space=pl.ANY)


def spread_kernel(
    query_hbm,
    key_hbm,
    value_hbm,
    lengths_hbm,
    placement_hbm,
    key_cache_hbm,
    value_cache_hbm,
    out_ref,
    own_ref,
    code_ref,
    query,
    key,
    value,
    lengths,
    placement,
    sems,
):
    pairs = (
        (query_hbm, query),
        (key_hbm, key),
        (value_hbm, value),
        (lengths_hbm, lengths),
        (placement_hbm, placement),
    )
    copies = [pltpu.make_async_copy(*pair, sems.at[i]) for i, pair in enumerate(pairs)]
    for copy in copies:
        copy.start()
    for copy in copies:
        copy.wait()
    wide = query[...].astype(jnp.float32)
    heads = [wide[:, head * HEAD_SIZE : (head + 1) * HEAD_SIZE] for head in range(GROUP)]
    heads = jnp.concatenate(heads, axis=0)
    out_ref[...] = jnp.broadcast_to(heads.astype(jnp.bfloat16)[None], out_ref.shape)
    score = SCALE * jnp.sum(heads * key[...].astype(jnp.float32), axis=-1, keepdims=True)
    device = lax.axis_index("attn")
    own = lax.broadcasted_iota(jnp.int32, out_ref.shape, 0) == device
    own_ref[0] = jnp.where(own, score[None], LOW)
    own_ref[1] = jnp.where(own, value[...].astype(jnp.float32)[None], 0.0)

    slots = code_ref.shape[0]
    places = placement[...] - device * slots
    row = lax.broadcasted_iota(jnp.int32, places.shape, 0)
    length = jnp.zeros_like(places)
    for r in range(lengths.shape[0]):
        length = jnp.where(row == r, lengths[r], length)
    start = lax.broadcasted_iota(jnp.int32, places.shape, 1) * BLOCK
    code = (row << LIVE_BITS) + jnp.clip(length - start, 0, BLOCK)
    for slot in range(slots):
        code_ref[slot] = jnp.sum(jnp.where(places == slot, code, 0))


def attention_kernel(
    code_ref,
    query_ref,
    own_ref,
    key_ref,
    value_ref,
    out_ref,
    scores,
    peaks,
    masses,
    sums,
):
    slots, block, _ = key_ref.shape
    rows = query_ref.shape[0]
    contract_last = (((1,), (1,)), ((), ()))
    position = lax.broadcasted_iota(jnp.int32, (GROUP, block), 1)
    lane = lax.broadcasted_iota(jnp.int32, (rows, GROUP, 128), 2)
    peaks[...] = own_ref[0]
    held = []
    for slot in range(slots):
        code = code_ref[slot]
        held.append((code >> LIVE_BITS, code & ((1 << LIVE_BITS) - 1)))
    for slot, (row, live) in enumerate(held):
        s = lax.dot_general(
            query_ref[row], key_ref[slot], contract_last, preferred_element_type=jnp.float32
        )
        s = jnp.where(position < live, s * SCALE, LOW)
        scores[slot] = s
        top = s[:, :128]
        for part in range(1, block // 128):
            top = jnp.maximum(top, s[:, part * 128 : (part + 1) * 128])
        peaks[row] = jnp.maximum(peaks[row], top)
    top = jnp.max(peaks[...], axis=-1, keepdims=True)
    top = top.astype(jnp.bfloat16).astype(jnp.float32)
    peaks[...] = jnp.broadcast_to(top, peaks.shape)
    own_weight = jnp.exp(own_ref[0] - peaks[...])
    masses[...] = jnp.where(lane == 0, own_weight, 0.0)
    sums[...] = own_weight.astype(jnp.bfloat16).astype(jnp.float32) * own_ref[1]
    for slot, (row, live) in enumerate(held):
        w = jnp.exp(scores[slot] - jnp.tile(peaks[row], (1, block // 128)))
        w = jnp.where(position < live, w, 0.0)
        mass = w[:, :128]
        for part in range(1, block // 128):
            mass = mass + w[:, part * 128 : (part + 1) * 128]
        masses[row] = masses[row] + mass
        sums[row] = sums[row] + jnp.dot(
            w.astype(jnp.bfloat16), value_ref[slot], preferred_element_type=jnp.float32
        )
    mass = jnp.sum(masses[...], axis=-1, keepdims=True)
    high = mass.astype(jnp.bfloat16).astype(jnp.float32)
    extra = jnp.where(lane == 0, peaks[...], jnp.where(lane == 1, high, mass - high))
    out_ref[...] = jnp.concatenate([sums[...], extra], axis=1).astype(jnp.bfloat16)


def finish_kernel(parts_ref, out_ref):
    parts = parts_ref[...].astype(jnp.float32)
    partial = parts[:, :GROUP]
    extra = parts[:, GROUP:]
    peaks = extra[:, :, 0:1]
    highest = jnp.max(peaks, axis=0, keepdims=True)
    factor = jnp.exp(peaks - highest)
    masses = extra[:, :, 1:2] + extra[:, :, 2:3]
    denominator = jnp.sum(masses * factor, axis=0)
    total = jnp.sum(partial * factor, axis=0)
    attended = (total / denominator).astype(jnp.bfloat16)
    out_ref[...] = jnp.broadcast_to(attended[None], out_ref.shape)


def project_kernel(attended_ref, w_ref, out_ref):
    heads = jnp.swapaxes(attended_ref[...].astype(jnp.float32), 0, 1).astype(jnp.bfloat16)
    total = None
    for head in range(GROUP):
        term = jnp.dot(
            heads[head],
            w_ref[head * HEAD_SIZE : (head + 1) * HEAD_SIZE, :],
            preferred_element_type=jnp.float32,
        )
        total = term if total is None else total + term
    ranks, packed, full = out_ref.shape
    width = total.shape[1] // ranks
    for rank in range(ranks):
        block = total[:, rank * width : (rank + 1) * width]
        out_ref[rank] = jnp.concatenate(
            [block[i * packed : (i + 1) * packed] for i in range(full // width)], axis=1
        )


def sum_kernel(terms_ref, out_ref):
    total = jnp.sum(terms_ref[...], axis=0)
    width = out_ref.shape[1]
    out_ref[...] = jnp.concatenate(
        [total[:, i * width : (i + 1) * width] for i in range(total.shape[1] // width)], axis=0
    ).astype(jnp.bfloat16)


def in_hbm(x):
    return pltpu.with_memory_space_constraint(x, pltpu.HBM)


def call(kernel, name, out_shape, in_specs, scratch_shapes=(), megabytes=2):
    return pl.pallas_call(
        kernel,
        out_shape=out_shape,
        in_specs=in_specs,
        out_specs=jax.tree.map(lambda _: VMEM, out_shape),
        scratch_shapes=scratch_shapes,
        compiler_params=pltpu.CompilerParams(vmem_limit_bytes=megabytes << 20),
        name=name,
    )


def shards(
    queries,
    fresh_keys,
    fresh_values,
    key_cache_blocks,
    value_cache_blocks,
    lengths,
    placement,
    w_out,
):
    rows = lengths.shape[0]
    slots, block, _ = key_cache_blocks.shape
    ranks = lax.axis_size("tensor")
    per_row = jax.ShapeDtypeStruct((rows, GROUP, HEAD_SIZE), jnp.bfloat16)

    small = (queries, fresh_keys, fresh_values, lengths, placement)
    room = [pltpu.VMEM(a.shape, a.dtype) for a in small]
    room[3] = pltpu.SMEM(lengths.shape, jnp.int32)
    spread, own, codes = pl.pallas_call(
        spread_kernel,
        out_shape=(
            per_row,
            jax.ShapeDtypeStruct((2, *per_row.shape), jnp.float32),
            pltpu.SMEM((slots,), jnp.int32),
        ),
        in_specs=[ANY] * (len(small) + 2),
        out_specs=(VMEM, VMEM, SMEM),
        scratch_shapes=room + [pltpu.SemaphoreType.DMA((len(small),))],
        compiler_params=pltpu.CompilerParams(vmem_limit_bytes=2 << 20),
        cost_estimate=pl.CostEstimate(
            flops=1 << 30, bytes_accessed=64 << 20, transcendentals=0
        ),
        name="spread",
    )(*map(in_hbm, (*small, key_cache_blocks, value_cache_blocks)))
    every_query = lax.all_to_all(spread, "attn", 0, 0, tiled=True)
    state = pltpu.VMEM((rows, GROUP, 128), jnp.float32)
    partials = call(
        attention_kernel,
        "attention",
        jax.ShapeDtypeStruct((rows, 2 * GROUP, HEAD_SIZE), jnp.bfloat16),
        [SMEM, VMEM, VMEM, VMEM, VMEM],
        [pltpu.VMEM((slots, GROUP, block), jnp.float32), state, state, state],
        4,
    )(codes, every_query, own, key_cache_blocks, value_cache_blocks)
    partials = lax.all_to_all(partials, "attn", 0, 0, tiled=True)
    attended = call(finish_kernel, "finish", per_row, [VMEM])(partials)
    attended = lax.all_to_all(attended, "attn", 0, 0, tiled=True)

    width = w_out.shape[1] // ranks
    terms = call(
        project_kernel,
        "project",
        jax.ShapeDtypeStruct((ranks, rows * width // 128, 128), jnp.float32),
        [VMEM, VMEM],
        (),
        4,
    )(attended, w_out)
    terms = lax.all_to_all(terms, "tensor", 0, 0, tiled=True)
    return call(sum_kernel, "sum", jax.ShapeDtypeStruct((rows, width), jnp.bfloat16), [VMEM])(terms)


def solution(mesh):
    return jax.shard_map(
        shards,
        mesh=mesh,
        in_specs=(
            P("attn", "tensor"),
            P("attn", "tensor"),
            P("attn", "tensor"),
            P("attn", None, "tensor"),
            P("attn", None, "tensor"),
            P(),
            P(),
            P("tensor", "attn"),
        ),
        out_specs=P(None, ("attn", "tensor")),
        check_vma=False,
    )
```

```python
import math

import jax
import jax.numpy as jnp
from jax import lax
from jax.experimental import pallas as pl
from jax.experimental.pallas import tpu as pltpu
from jax.sharding import PartitionSpec as P

QUERY_HEADS = 64
KEY_VALUE_HEADS = 8
HEAD_SIZE = 128
BLOCK = 512
GROUP = QUERY_HEADS // KEY_VALUE_HEADS
SCALE = 1.0 / math.sqrt(HEAD_SIZE)
LOW = -(2.0**99)
FAR = 18
FAR_RANK = 4
LIVE_BITS = 10

VMEM = pl.BlockSpec(memory_space=pltpu.VMEM)
SMEM = pl.BlockSpec(memory_space=pltpu.SMEM)
ANY = pl.BlockSpec(memory_space=pl.ANY)


def spread_kernel(
    query_hbm,
    key_hbm,
    value_hbm,
    lengths_hbm,
    placement_hbm,
    key_cache_hbm,
    value_cache_hbm,
    out_ref,
    own_ref,
    code_ref,
    query,
    key,
    value,
    lengths,
    placement,
    sems,
):
    pairs = (
        (query_hbm, query),
        (key_hbm, key),
        (value_hbm, value),
        (lengths_hbm, lengths),
        (placement_hbm, placement),
    )
    copies = [pltpu.make_async_copy(*pair, sems.at[i]) for i, pair in enumerate(pairs)]
    for copy in copies:
        copy.start()
    for copy in copies:
        copy.wait()
    wide = query[...].astype(jnp.float32)
    heads = [wide[:, head * HEAD_SIZE : (head + 1) * HEAD_SIZE] for head in range(GROUP)]
    heads = jnp.concatenate(heads, axis=0)
    out_ref[...] = jnp.broadcast_to(heads.astype(jnp.bfloat16)[None], out_ref.shape)
    score = SCALE * jnp.sum(heads * key[...].astype(jnp.float32), axis=-1, keepdims=True)
    device = lax.axis_index("attn")
    own = lax.broadcasted_iota(jnp.int32, out_ref.shape, 0) == device ^ FAR
    own_ref[0] = jnp.where(own, score[None], LOW)
    own_ref[1] = jnp.where(own, value[...].astype(jnp.float32)[None], 0.0)

    slots = code_ref.shape[0]
    places = placement[...] - device * slots
    row = lax.broadcasted_iota(jnp.int32, places.shape, 0)
    length = jnp.zeros_like(places)
    for r in range(lengths.shape[0]):
        length = jnp.where(row == r, lengths[r], length)
    start = lax.broadcasted_iota(jnp.int32, places.shape, 1) * BLOCK
    code = ((row ^ FAR) << LIVE_BITS) + jnp.clip(length - start, 0, BLOCK)
    for slot in range(slots):
        code_ref[slot] = jnp.sum(jnp.where(places == slot, code, 0))


def attention_kernel(
    code_ref,
    query_ref,
    own_ref,
    key_ref,
    value_ref,
    out_ref,
    scores,
    peaks,
    masses,
    sums,
):
    slots, block, _ = key_ref.shape
    rows = query_ref.shape[0]
    contract_last = (((1,), (1,)), ((), ()))
    position = lax.broadcasted_iota(jnp.int32, (GROUP, block), 1)
    lane = lax.broadcasted_iota(jnp.int32, (rows, GROUP, 128), 2)
    peaks[...] = own_ref[0]
    held = []
    for slot in range(slots):
        code = code_ref[slot]
        held.append((code >> LIVE_BITS, code & ((1 << LIVE_BITS) - 1)))
    for slot, (row, live) in enumerate(held):
        s = lax.dot_general(
            query_ref[row], key_ref[slot], contract_last, preferred_element_type=jnp.float32
        )
        s = jnp.where(position < live, s * SCALE, LOW)
        scores[slot] = s
        top = s[:, :128]
        for part in range(1, block // 128):
            top = jnp.maximum(top, s[:, part * 128 : (part + 1) * 128])
        peaks[row] = jnp.maximum(peaks[row], top)
    top = jnp.max(peaks[...], axis=-1, keepdims=True)
    top = top.astype(jnp.bfloat16).astype(jnp.float32)
    peaks[...] = jnp.broadcast_to(top, peaks.shape)
    own_weight = jnp.exp(own_ref[0] - peaks[...])
    masses[...] = jnp.where(lane == 0, own_weight, 0.0)
    sums[...] = own_weight.astype(jnp.bfloat16).astype(jnp.float32) * own_ref[1]
    for slot, (row, live) in enumerate(held):
        w = jnp.exp(scores[slot] - jnp.tile(peaks[row], (1, block // 128)))
        w = jnp.where(position < live, w, 0.0)
        mass = w[:, :128]
        for part in range(1, block // 128):
            mass = mass + w[:, part * 128 : (part + 1) * 128]
        masses[row] = masses[row] + mass
        sums[row] = sums[row] + jnp.dot(
            w.astype(jnp.bfloat16), value_ref[slot], preferred_element_type=jnp.float32
        )
    mass = jnp.sum(masses[...], axis=-1, keepdims=True)
    high = mass.astype(jnp.bfloat16).astype(jnp.float32)
    extra = jnp.where(lane == 0, peaks[...], jnp.where(lane == 1, high, mass - high))
    out_ref[...] = jnp.concatenate([sums[...], extra], axis=1).astype(jnp.bfloat16)


def finish_kernel(parts_ref, out_ref):
    parts = parts_ref[...].astype(jnp.float32)
    partial = parts[:, :GROUP]
    extra = parts[:, GROUP:]
    peaks = extra[:, :, 0:1]
    highest = jnp.max(peaks, axis=0, keepdims=True)
    factor = jnp.exp(peaks - highest)
    masses = extra[:, :, 1:2] + extra[:, :, 2:3]
    denominator = jnp.sum(masses * factor, axis=0)
    total = jnp.sum(partial * factor, axis=0)
    attended = (total / denominator).astype(jnp.bfloat16)
    out_ref[...] = jnp.broadcast_to(attended[None], out_ref.shape)


def project_kernel(attended_ref, w_ref, out_ref):
    heads = jnp.swapaxes(attended_ref[...].astype(jnp.float32), 0, 1).astype(jnp.bfloat16)
    total = None
    for head in range(GROUP):
        term = jnp.dot(
            heads[head],
            w_ref[head * HEAD_SIZE : (head + 1) * HEAD_SIZE, :],
            preferred_element_type=jnp.float32,
        )
        total = term if total is None else total + term
    ranks, packed, full = out_ref.shape
    width = total.shape[1] // ranks
    for rank in range(ranks):
        block = total[:, rank * width : (rank + 1) * width]
        out_ref[rank ^ FAR_RANK] = jnp.concatenate(
            [block[i * packed : (i + 1) * packed] for i in range(full // width)], axis=1
        )


def sum_kernel(terms_ref, out_ref):
    total = jnp.sum(terms_ref[...], axis=0)
    rows, width = out_ref.shape
    packed = total.shape[0]
    low = FAR % packed
    step = low & -low
    total = jnp.concatenate(
        [total[i ^ low : (i ^ low) + step] for i in range(0, packed, step)], axis=0
    )
    blocks = [(i ^ FAR // packed) * width for i in range(rows // packed)]
    out_ref[...] = jnp.concatenate([total[:, at : at + width] for at in blocks], axis=0).astype(
        jnp.bfloat16
    )


def exchange(x, axis, far):
    order = [i ^ far for i in range(lax.axis_size(axis))]
    return lax.all_to_all(x, axis, 0, 0, tiled=True, axis_index_groups=[order])


def in_hbm(x):
    return pltpu.with_memory_space_constraint(x, pltpu.HBM)


def call(kernel, name, out_shape, in_specs, scratch_shapes=(), megabytes=2):
    return pl.pallas_call(
        kernel,
        out_shape=out_shape,
        in_specs=in_specs,
        out_specs=jax.tree.map(lambda _: VMEM, out_shape),
        scratch_shapes=scratch_shapes,
        compiler_params=pltpu.CompilerParams(vmem_limit_bytes=megabytes << 20),
        name=name,
    )


def shards(
    queries,
    fresh_keys,
    fresh_values,
    key_cache_blocks,
    value_cache_blocks,
    lengths,
    placement,
    w_out,
):
    rows = lengths.shape[0]
    slots, block, _ = key_cache_blocks.shape
    ranks = lax.axis_size("tensor")
    per_row = jax.ShapeDtypeStruct((rows, GROUP, HEAD_SIZE), jnp.bfloat16)

    small = (queries, fresh_keys, fresh_values, lengths, placement)
    room = [pltpu.VMEM(a.shape, a.dtype) for a in small]
    room[3] = pltpu.SMEM(lengths.shape, jnp.int32)
    spread, own, codes = pl.pallas_call(
        spread_kernel,
        out_shape=(
            per_row,
            jax.ShapeDtypeStruct((2, *per_row.shape), jnp.float32),
            pltpu.SMEM((slots,), jnp.int32),
        ),
        in_specs=[ANY] * (len(small) + 2),
        out_specs=(VMEM, VMEM, SMEM),
        scratch_shapes=room + [pltpu.SemaphoreType.DMA((len(small),))],
        compiler_params=pltpu.CompilerParams(vmem_limit_bytes=2 << 20),
        cost_estimate=pl.CostEstimate(
            flops=1 << 30, bytes_accessed=64 << 20, transcendentals=0
        ),
        name="spread",
    )(*map(in_hbm, (*small, key_cache_blocks, value_cache_blocks)))
    every_query = exchange(spread, "attn", FAR)
    state = pltpu.VMEM((rows, GROUP, 128), jnp.float32)
    partials = call(
        attention_kernel,
        "attention",
        jax.ShapeDtypeStruct((rows, 2 * GROUP, HEAD_SIZE), jnp.bfloat16),
        [SMEM, VMEM, VMEM, VMEM, VMEM],
        [pltpu.VMEM((slots, GROUP, block), jnp.float32), state, state, state],
        4,
    )(codes, every_query, own, key_cache_blocks, value_cache_blocks)
    partials = exchange(partials, "attn", FAR)
    attended = call(finish_kernel, "finish", per_row, [VMEM])(partials)
    attended = exchange(attended, "attn", FAR)

    width = w_out.shape[1] // ranks
    terms = call(
        project_kernel,
        "project",
        jax.ShapeDtypeStruct((ranks, rows * width // 128, 128), jnp.float32),
        [VMEM, VMEM],
        (),
        4,
    )(attended, w_out)
    terms = exchange(terms, "tensor", FAR_RANK)
    return call(sum_kernel, "sum", jax.ShapeDtypeStruct((rows, width), jnp.bfloat16), [VMEM])(terms)


def solution(mesh):
    return jax.shard_map(
        shards,
        mesh=mesh,
        in_specs=(
            P("attn", "tensor"),
            P("attn", "tensor"),
            P("attn", "tensor"),
            P("attn", None, "tensor"),
            P("attn", None, "tensor"),
            P(),
            P(),
            P("tensor", "attn"),
        ),
        out_specs=P(None, ("attn", "tensor")),
        check_vma=False,
    )
```

```python
import math

import jax
import jax.numpy as jnp
from jax import lax
from jax.experimental import pallas as pl
from jax.experimental.pallas import tpu as pltpu
from jax.sharding import PartitionSpec as P

QUERY_HEADS = 64
KEY_VALUE_HEADS = 8
HEAD_SIZE = 128
BLOCK = 512
GROUP = QUERY_HEADS // KEY_VALUE_HEADS
SCALE = 1.0 / math.sqrt(HEAD_SIZE)
LOW = -(2.0**99)
FAR = 18
FAR_RANK = 4
LIVE_BITS = 10
CODE_BITS = LIVE_BITS + 5

VMEM = pl.BlockSpec(memory_space=pltpu.VMEM)
SMEM = pl.BlockSpec(memory_space=pltpu.SMEM)
ANY = pl.BlockSpec(memory_space=pl.ANY)


def spread_kernel(
    query_hbm,
    key_hbm,
    value_hbm,
    lengths_hbm,
    placement_hbm,
    out_ref,
    own_ref,
    code_ref,
    query,
    key,
    value,
    lengths,
    placement,
    sems,
):
    pairs = (
        (query_hbm, query),
        (key_hbm, key),
        (value_hbm, value),
        (lengths_hbm, lengths),
        (placement_hbm, placement),
    )
    copies = [pltpu.make_async_copy(*pair, sems.at[i]) for i, pair in enumerate(pairs)]
    for copy in copies:
        copy.start()
    for copy in copies:
        copy.wait()
    wide = query[...].astype(jnp.float32)
    heads = [wide[:, head * HEAD_SIZE : (head + 1) * HEAD_SIZE] for head in range(GROUP)]
    heads = jnp.concatenate(heads, axis=0)
    out_ref[...] = jnp.broadcast_to(heads.astype(jnp.bfloat16)[None], out_ref.shape)
    score = SCALE * jnp.sum(heads * key[...].astype(jnp.float32), axis=-1, keepdims=True)
    device = lax.axis_index("attn")
    own = lax.broadcasted_iota(jnp.int32, out_ref.shape, 0) == device ^ FAR
    own_ref[0] = jnp.where(own, score[None], LOW)
    own_ref[1] = jnp.where(own, value[...].astype(jnp.float32)[None], 0.0)

    slots = code_ref.shape[0]
    places = placement[...] - device * slots
    row = lax.broadcasted_iota(jnp.int32, places.shape, 0)
    length = jnp.zeros_like(places)
    for r in range(lengths.shape[0]):
        length = jnp.where(row == r, lengths[r], length)
    start = lax.broadcasted_iota(jnp.int32, places.shape, 1) * BLOCK
    code = ((row ^ FAR) << LIVE_BITS) + jnp.clip(length - start, 0, BLOCK)
    high = code << CODE_BITS
    for slot in range(0, slots, 2):
        both = jnp.sum(jnp.where(places == slot, code, jnp.where(places == slot + 1, high, 0)))
        code_ref[slot] = both & ((1 << CODE_BITS) - 1)
        code_ref[slot + 1] = both >> CODE_BITS


def hold_kernel(spread_ref, key_cache_hbm, value_cache_hbm, out_ref):
    pass


def attention_kernel(
    code_ref,
    query_ref,
    own_ref,
    key_ref,
    value_ref,
    out_ref,
    scores,
    peaks,
    masses,
    sums,
):
    slots, block, _ = key_ref.shape
    rows = query_ref.shape[0]
    contract_last = (((1,), (1,)), ((), ()))
    position = lax.broadcasted_iota(jnp.int32, (GROUP, block), 1)
    lane = lax.broadcasted_iota(jnp.int32, (rows, GROUP, 128), 2)
    peaks[...] = own_ref[0]
    held = []
    for slot in range(slots):
        code = code_ref[slot]
        held.append((code >> LIVE_BITS, code & ((1 << LIVE_BITS) - 1)))
    for slot, (row, live) in enumerate(held):
        s = lax.dot_general(
            query_ref[row], key_ref[slot], contract_last, preferred_element_type=jnp.float32
        )
        s = jnp.where(position < live, s * SCALE, LOW)
        scores[slot] = s
        top = s[:, :128]
        for part in range(1, block // 128):
            top = jnp.maximum(top, s[:, part * 128 : (part + 1) * 128])
        peaks[row] = jnp.maximum(peaks[row], top)
    top = jnp.max(peaks[...], axis=-1, keepdims=True)
    top = top.astype(jnp.bfloat16).astype(jnp.float32)
    peaks[...] = jnp.broadcast_to(top, peaks.shape)
    own_weight = jnp.exp(own_ref[0] - peaks[...])
    masses[...] = jnp.where(lane == 0, own_weight, 0.0)
    sums[...] = own_weight.astype(jnp.bfloat16).astype(jnp.float32) * own_ref[1]
    for slot, (row, _) in enumerate(held):
        w = jnp.exp(scores[slot] - jnp.tile(peaks[row], (1, block // 128)))
        mass = w[:, :128]
        for part in range(1, block // 128):
            mass = mass + w[:, part * 128 : (part + 1) * 128]
        masses[row] = masses[row] + mass
        sums[row] = sums[row] + jnp.dot(
            w.astype(jnp.bfloat16), value_ref[slot], preferred_element_type=jnp.float32
        )
    mass = jnp.sum(masses[...], axis=-1, keepdims=True)
    high = mass.astype(jnp.bfloat16).astype(jnp.float32)
    extra = jnp.where(lane == 0, peaks[...], jnp.where(lane == 1, high, mass - high))
    out_ref[...] = jnp.concatenate([sums[...], extra], axis=1).astype(jnp.bfloat16)


def finish_kernel(parts_ref, out_ref):
    parts = parts_ref[...].astype(jnp.float32)
    partial = parts[:, :GROUP]
    extra = parts[:, GROUP:]
    peaks = extra[:, :, 0:1]
    highest = jnp.max(peaks, axis=0, keepdims=True)
    factor = jnp.exp(peaks - highest)
    masses = extra[:, :, 1:2] + extra[:, :, 2:3]
    denominator = jnp.sum(masses * factor, axis=0)
    total = jnp.sum(partial * factor, axis=0)
    attended = (total / denominator).astype(jnp.bfloat16)
    out_ref[...] = jnp.broadcast_to(attended[None], out_ref.shape)


def project_kernel(attended_ref, w_ref, out_ref):
    rows = [attended_ref[row ^ FAR].astype(jnp.float32) for row in range(attended_ref.shape[0])]
    heads = jnp.swapaxes(jnp.stack(rows), 0, 1).astype(jnp.bfloat16)
    total = None
    for head in range(GROUP):
        term = jnp.dot(
            heads[head],
            w_ref[head * HEAD_SIZE : (head + 1) * HEAD_SIZE, :],
            preferred_element_type=jnp.float32,
        )
        total = term if total is None else total + term
    ranks, packed, full = out_ref.shape
    width = total.shape[1] // ranks
    for rank in range(ranks):
        block = total[:, rank * width : (rank + 1) * width]
        out_ref[rank ^ FAR_RANK] = jnp.concatenate(
            [block[i * packed : (i + 1) * packed] for i in range(full // width)], axis=1
        )


def sum_kernel(terms_ref, out_ref):
    total = jnp.sum(terms_ref[...], axis=0)
    width = out_ref.shape[1]
    out_ref[...] = jnp.concatenate(
        [total[:, i * width : (i + 1) * width] for i in range(total.shape[1] // width)], axis=0
    ).astype(jnp.bfloat16)


def exchange(x, axis, far):
    order = [i ^ far for i in range(lax.axis_size(axis))]
    return lax.all_to_all(x, axis, 0, 0, tiled=True, axis_index_groups=[order])


def in_hbm(x):
    return pltpu.with_memory_space_constraint(x, pltpu.HBM)


def call(kernel, name, out_shape, in_specs, scratch_shapes=(), megabytes=2):
    return pl.pallas_call(
        kernel,
        out_shape=out_shape,
        in_specs=in_specs,
        out_specs=jax.tree.map(lambda _: VMEM, out_shape),
        scratch_shapes=scratch_shapes,
        compiler_params=pltpu.CompilerParams(vmem_limit_bytes=megabytes << 20),
        name=name,
    )


def shards(
    queries,
    fresh_keys,
    fresh_values,
    key_cache_blocks,
    value_cache_blocks,
    lengths,
    placement,
    w_out,
):
    rows = lengths.shape[0]
    slots, block, _ = key_cache_blocks.shape
    ranks = lax.axis_size("tensor")
    per_row = jax.ShapeDtypeStruct((rows, GROUP, HEAD_SIZE), jnp.bfloat16)

    small = (queries, fresh_keys, fresh_values, lengths, placement)
    room = [pltpu.VMEM(a.shape, a.dtype) for a in small]
    room[3] = pltpu.SMEM(lengths.shape, jnp.int32)
    spread, own, codes = pl.pallas_call(
        spread_kernel,
        out_shape=(
            per_row,
            jax.ShapeDtypeStruct((2, *per_row.shape), jnp.float32),
            pltpu.SMEM((slots,), jnp.int32),
        ),
        in_specs=[ANY] * len(small),
        out_specs=(VMEM, VMEM, SMEM),
        scratch_shapes=room + [pltpu.SemaphoreType.DMA((len(small),))],
        compiler_params=pltpu.CompilerParams(vmem_limit_bytes=2 << 20),
        name="spread",
    )(*map(in_hbm, small))
    spread = pl.pallas_call(
        hold_kernel,
        out_shape=per_row,
        in_specs=[VMEM, ANY, ANY],
        out_specs=VMEM,
        input_output_aliases={0: 0},
        compiler_params=pltpu.CompilerParams(vmem_limit_bytes=2 << 20),
        name="hold",
    )(spread, in_hbm(key_cache_blocks), in_hbm(value_cache_blocks))
    every_query = exchange(spread, "attn", FAR)
    state = pltpu.VMEM((rows, GROUP, 128), jnp.float32)
    partials = call(
        attention_kernel,
        "attention",
        jax.ShapeDtypeStruct((rows, 2 * GROUP, HEAD_SIZE), jnp.bfloat16),
        [SMEM, VMEM, VMEM, VMEM, VMEM],
        [pltpu.VMEM((slots, GROUP, block), jnp.float32), state, state, state],
        4,
    )(codes, every_query, own, key_cache_blocks, value_cache_blocks)
    partials = exchange(partials, "attn", FAR)
    attended = call(finish_kernel, "finish", per_row, [VMEM])(partials)
    attended = exchange(attended, "attn", FAR)

    width = w_out.shape[1] // ranks
    terms = call(
        project_kernel,
        "project",
        jax.ShapeDtypeStruct((ranks, rows * width // 128, 128), jnp.float32),
        [VMEM, VMEM],
        (),
        4,
    )(attended, w_out)
    terms = exchange(terms, "tensor", FAR_RANK)
    return call(sum_kernel, "sum", jax.ShapeDtypeStruct((rows, width), jnp.bfloat16), [VMEM])(terms)


def solution(mesh):
    return jax.shard_map(
        shards,
        mesh=mesh,
        in_specs=(
            P("attn", "tensor"),
            P("attn", "tensor"),
            P("attn", "tensor"),
            P("attn", None, "tensor"),
            P("attn", None, "tensor"),
            P(),
            P(),
            P("tensor", "attn"),
        ),
        out_specs=P(None, ("attn", "tensor")),
        check_vma=False,
    )
```

```python
import math

import jax
import jax.numpy as jnp
from jax import lax
from jax.experimental import pallas as pl
from jax.experimental.pallas import tpu as pltpu
from jax.sharding import PartitionSpec as P

QUERY_HEADS = 64
KEY_VALUE_HEADS = 8
HEAD_SIZE = 128
BLOCK = 512
GROUP = QUERY_HEADS // KEY_VALUE_HEADS
SCALE = 1.0 / math.sqrt(HEAD_SIZE)
LOW = -(2.0**99)
FAR = 18
FAR_RANK = 4
X = 4
SETS = 2 * X
FAR_SET = 6
LIVE_BITS = 10
CODE_BITS = LIVE_BITS + 5

VMEM = pl.BlockSpec(memory_space=pltpu.VMEM)
SMEM = pl.BlockSpec(memory_space=pltpu.SMEM)
ANY = pl.BlockSpec(memory_space=pl.ANY)


def spread_kernel(
    query_hbm,
    key_hbm,
    value_hbm,
    lengths_hbm,
    placement_hbm,
    out_ref,
    own_ref,
    code_ref,
    query,
    key,
    value,
    lengths,
    placement,
    sems,
):
    pairs = (
        (query_hbm, query),
        (key_hbm, key),
        (value_hbm, value),
        (lengths_hbm, lengths),
        (placement_hbm, placement),
    )
    copies = [pltpu.make_async_copy(*pair, sems.at[i]) for i, pair in enumerate(pairs)]
    for copy in copies:
        copy.start()
    for copy in copies:
        copy.wait()
    wide = query[...].astype(jnp.float32)
    heads = [wide[:, head * HEAD_SIZE : (head + 1) * HEAD_SIZE] for head in range(GROUP)]
    heads = jnp.concatenate(heads, axis=0)
    out_ref[...] = jnp.broadcast_to(heads.astype(jnp.bfloat16)[None], out_ref.shape)
    score = SCALE * jnp.sum(heads * key[...].astype(jnp.float32), axis=-1, keepdims=True)
    device = lax.axis_index("attn")
    own = lax.broadcasted_iota(jnp.int32, out_ref.shape, 0) == device ^ FAR
    own_ref[0] = jnp.where(own, score[None], LOW)
    own_ref[1] = jnp.where(own, value[...].astype(jnp.float32)[None], 0.0)

    slots = code_ref.shape[0]
    places = placement[...] - device * slots
    row = lax.broadcasted_iota(jnp.int32, places.shape, 0)
    length = jnp.zeros_like(places)
    for r in range(lengths.shape[0]):
        length = jnp.where(row == r, lengths[r], length)
    start = lax.broadcasted_iota(jnp.int32, places.shape, 1) * BLOCK
    code = ((row ^ FAR) << LIVE_BITS) + jnp.clip(length - start, 0, BLOCK)
    high = code << CODE_BITS
    for slot in range(0, slots, 2):
        both = jnp.sum(jnp.where(places == slot, code, jnp.where(places == slot + 1, high, 0)))
        code_ref[slot] = both & ((1 << CODE_BITS) - 1)
        code_ref[slot + 1] = both >> CODE_BITS


def hold_kernel(spread_ref, key_cache_hbm, value_cache_hbm, out_ref):
    pass


def attention_kernel(
    code_ref,
    query_ref,
    own_ref,
    key_ref,
    value_ref,
    out_ref,
    scores,
    peaks,
    masses,
    sums,
):
    slots, block, _ = key_ref.shape
    rows = query_ref.shape[0]
    contract_last = (((1,), (1,)), ((), ()))
    position = lax.broadcasted_iota(jnp.int32, (GROUP, block), 1)
    lane = lax.broadcasted_iota(jnp.int32, (rows, GROUP, 128), 2)
    peaks[...] = own_ref[0]
    held = []
    for slot in range(slots):
        code = code_ref[slot]
        held.append((code >> LIVE_BITS, code & ((1 << LIVE_BITS) - 1)))
    for slot, (row, live) in enumerate(held):
        s = lax.dot_general(
            query_ref[row], key_ref[slot], contract_last, preferred_element_type=jnp.float32
        )
        s = jnp.where(position < live, s * SCALE, LOW)
        scores[slot] = s
        top = s[:, :128]
        for part in range(1, block // 128):
            top = jnp.maximum(top, s[:, part * 128 : (part + 1) * 128])
        peaks[row] = jnp.maximum(peaks[row], top)
    top = jnp.max(peaks[...], axis=-1, keepdims=True)
    top = top.astype(jnp.bfloat16).astype(jnp.float32)
    peaks[...] = jnp.broadcast_to(top, peaks.shape)
    own_weight = jnp.exp(own_ref[0] - peaks[...])
    masses[...] = jnp.where(lane == 0, own_weight, 0.0)
    sums[...] = own_weight.astype(jnp.bfloat16).astype(jnp.float32) * own_ref[1]
    for slot, (row, _) in enumerate(held):
        w = jnp.exp(scores[slot] - jnp.tile(peaks[row], (1, block // 128)))
        mass = w[:, :128]
        for part in range(1, block // 128):
            mass = mass + w[:, part * 128 : (part + 1) * 128]
        masses[row] = masses[row] + mass
        sums[row] = sums[row] + jnp.dot(
            w.astype(jnp.bfloat16), value_ref[slot], preferred_element_type=jnp.float32
        )
    mass = jnp.sum(masses[...], axis=-1, keepdims=True)
    high = mass.astype(jnp.bfloat16).astype(jnp.float32)
    low = mass - high
    lane = lane[0]
    share = rows // SETS
    for which in range(SETS):
        extra = jnp.zeros((GROUP, 128), jnp.float32)
        for i in range(share):
            place, at = which * share + i, i * (128 // share)
            extra = jnp.where(lane == at, peaks[place], extra)
            extra = jnp.where(lane == at + 1, high[place], extra)
            extra = jnp.where(lane == at + 2, low[place], extra)
        block = sums[which * share : (which + 1) * share].reshape(share * GROUP, 128)
        block = jnp.concatenate([block, extra], axis=0).astype(jnp.bfloat16)
        for place in range(out_ref.shape[0]):
            if set_of(place ^ FAR) == which:
                out_ref[place] = block


def set_of(device):
    return device // X % 2 * X + device % X


def finish_kernel(parts_ref, out_ref):
    parts = parts_ref[...].astype(jnp.float32)
    share = parts.shape[1] // GROUP - 1
    extra = parts[:, share * GROUP :]
    attended = []
    for i in range(share):
        partial = parts[:, i * GROUP : (i + 1) * GROUP]
        at = i * (128 // share)
        peaks = extra[:, :, at : at + 1]
        highest = jnp.max(peaks, axis=0, keepdims=True)
        factor = jnp.exp(peaks - highest)
        masses = extra[:, :, at + 1 : at + 2] + extra[:, :, at + 2 : at + 3]
        denominator = jnp.sum(masses * factor, axis=0)
        attended.append(jnp.sum(partial * factor, axis=0) / denominator)
    attended = jnp.concatenate(attended, axis=0).astype(jnp.bfloat16)
    out_ref[...] = jnp.broadcast_to(attended[None], out_ref.shape)


def project_kernel(attended_ref, w_ref, out_ref):
    sets = attended_ref[...].astype(jnp.float32)
    share = sets.shape[1] // GROUP
    rows = []
    for place in (row ^ FAR for row in range(SETS * share)):
        at = place % share * GROUP
        rows.append(sets[place // share ^ FAR_SET, at : at + GROUP])
    heads = jnp.swapaxes(jnp.stack(rows), 0, 1).astype(jnp.bfloat16)
    total = None
    for head in range(GROUP):
        term = jnp.dot(
            heads[head],
            w_ref[head * HEAD_SIZE : (head + 1) * HEAD_SIZE, :],
            preferred_element_type=jnp.float32,
        )
        total = term if total is None else total + term
    ranks, packed, full = out_ref.shape
    width = total.shape[1] // ranks
    for rank in range(ranks):
        block = total[:, rank * width : (rank + 1) * width]
        out_ref[rank ^ FAR_RANK] = jnp.concatenate(
            [block[i * packed : (i + 1) * packed] for i in range(full // width)], axis=1
        )


def sum_kernel(terms_ref, out_ref):
    total = jnp.sum(terms_ref[...], axis=0)
    width = out_ref.shape[1]
    out_ref[...] = jnp.concatenate(
        [total[:, i * width : (i + 1) * width] for i in range(total.shape[1] // width)], axis=0
    ).astype(jnp.bfloat16)


def exchange(x, axis, groups):
    return lax.all_to_all(x, axis, 0, 0, tiled=True, axis_index_groups=groups)


def in_hbm(x):
    return pltpu.with_memory_space_constraint(x, pltpu.HBM)


def call(kernel, name, out_shape, in_specs, scratch_shapes=(), megabytes=2):
    return pl.pallas_call(
        kernel,
        out_shape=out_shape,
        in_specs=in_specs,
        out_specs=jax.tree.map(lambda _: VMEM, out_shape),
        scratch_shapes=scratch_shapes,
        compiler_params=pltpu.CompilerParams(vmem_limit_bytes=megabytes << 20),
        name=name,
    )


def shards(
    queries,
    fresh_keys,
    fresh_values,
    key_cache_blocks,
    value_cache_blocks,
    lengths,
    placement,
    w_out,
):
    rows = lengths.shape[0]
    slots, block, _ = key_cache_blocks.shape
    ranks = lax.axis_size("tensor")
    everyone = [[i ^ FAR for i in range(rows)]]
    blocks = [[at + (i ^ FAR_SET) for i in range(SETS)] for at in range(0, rows, SETS)]
    share = rows // SETS * GROUP
    per_row = jax.ShapeDtypeStruct((rows, GROUP, HEAD_SIZE), jnp.bfloat16)

    small = (queries, fresh_keys, fresh_values, lengths, placement)
    room = [pltpu.VMEM(a.shape, a.dtype) for a in small]
    room[3] = pltpu.SMEM(lengths.shape, jnp.int32)
    spread, own, codes = pl.pallas_call(
        spread_kernel,
        out_shape=(
            per_row,
            jax.ShapeDtypeStruct((2, *per_row.shape), jnp.float32),
            pltpu.SMEM((slots,), jnp.int32),
        ),
        in_specs=[ANY] * len(small),
        out_specs=(VMEM, VMEM, SMEM),
        scratch_shapes=room + [pltpu.SemaphoreType.DMA((len(small),))],
        compiler_params=pltpu.CompilerParams(vmem_limit_bytes=2 << 20),
        name="spread",
    )(*map(in_hbm, small))
    spread = pl.pallas_call(
        hold_kernel,
        out_shape=per_row,
        in_specs=[VMEM, ANY, ANY],
        out_specs=VMEM,
        input_output_aliases={0: 0},
        compiler_params=pltpu.CompilerParams(vmem_limit_bytes=2 << 20),
        name="hold",
    )(spread, in_hbm(key_cache_blocks), in_hbm(value_cache_blocks))
    every_query = exchange(spread, "attn", everyone)
    state = pltpu.VMEM((rows, GROUP, 128), jnp.float32)
    partials = call(
        attention_kernel,
        "attention",
        jax.ShapeDtypeStruct((rows, share + GROUP, HEAD_SIZE), jnp.bfloat16),
        [SMEM, VMEM, VMEM, VMEM, VMEM],
        [pltpu.VMEM((slots, GROUP, block), jnp.float32), state, state, state],
        4,
    )(codes, every_query, own, key_cache_blocks, value_cache_blocks)
    partials = exchange(partials, "attn", everyone)
    attended = call(
        finish_kernel,
        "finish",
        jax.ShapeDtypeStruct((SETS, share, HEAD_SIZE), jnp.bfloat16),
        [VMEM],
    )(partials)
    attended = exchange(attended, "attn", blocks)

    width = w_out.shape[1] // ranks
    terms = call(
        project_kernel,
        "project",
        jax.ShapeDtypeStruct((ranks, rows * width // 128, 128), jnp.float32),
        [VMEM, VMEM],
        (),
        4,
    )(attended, w_out)
    terms = exchange(terms, "tensor", [[i ^ FAR_RANK for i in range(ranks)]])
    return call(sum_kernel, "sum", jax.ShapeDtypeStruct((rows, width), jnp.bfloat16), [VMEM])(terms)


def solution(mesh):
    return jax.shard_map(
        shards,
        mesh=mesh,
        in_specs=(
            P("attn", "tensor"),
            P("attn", "tensor"),
            P("attn", "tensor"),
            P("attn", None, "tensor"),
            P("attn", None, "tensor"),
            P(),
            P(),
            P("tensor", "attn"),
        ),
        out_specs=P(None, ("attn", "tensor")),
        check_vma=False,
    )
```

```python
import math

import jax
import jax.numpy as jnp
from jax import lax
from jax.experimental import pallas as pl
from jax.experimental.pallas import tpu as pltpu
from jax.sharding import PartitionSpec as P

QUERY_HEADS = 64
KEY_VALUE_HEADS = 8
HEAD_SIZE = 128
BLOCK = 512
GROUP = QUERY_HEADS // KEY_VALUE_HEADS
SCALE = 1.0 / math.sqrt(HEAD_SIZE)
LOW = -(2.0**99)
FAR_RANK = 4
Z = 8
X = 4


def hops(device):
    return abs(device // X - Z // 2) + abs(device % X - X // 2)


ORDER = sorted(range(Z * X), key=lambda device: (hops(device), device))
PLACE = [ORDER.index(device) for device in range(Z * X)]

SETS = 2 * X
FAR_SET = 6
LIVE_BITS = 10
CODE_BITS = LIVE_BITS + 5

VMEM = pl.BlockSpec(memory_space=pltpu.VMEM)
SMEM = pl.BlockSpec(memory_space=pltpu.SMEM)
ANY = pl.BlockSpec(memory_space=pl.ANY)


def spread_kernel(
    query_hbm,
    key_hbm,
    value_hbm,
    lengths_hbm,
    placement_hbm,
    out_ref,
    own_ref,
    code_ref,
    query,
    key,
    value,
    lengths,
    placement,
    sems,
):
    pairs = (
        (query_hbm, query),
        (key_hbm, key),
        (value_hbm, value),
        (lengths_hbm, lengths),
        (placement_hbm, placement),
    )
    copies = [pltpu.make_async_copy(*pair, sems.at[i]) for i, pair in enumerate(pairs)]
    for copy in copies:
        copy.start()
    for copy in copies:
        copy.wait()
    wide = query[...].astype(jnp.float32)
    heads = [wide[:, head * HEAD_SIZE : (head + 1) * HEAD_SIZE] for head in range(GROUP)]
    heads = jnp.concatenate(heads, axis=0)
    out_ref[...] = jnp.broadcast_to(heads.astype(jnp.bfloat16)[None], out_ref.shape)
    score = SCALE * jnp.sum(heads * key[...].astype(jnp.float32), axis=-1, keepdims=True)
    device = lax.axis_index("attn")
    score = jnp.broadcast_to(score, (GROUP, HEAD_SIZE))
    fresh = jnp.broadcast_to(value[...].astype(jnp.float32), (GROUP, HEAD_SIZE))
    for place, owner in enumerate(ORDER):
        own_ref[0, place] = jnp.where(device == owner, score, LOW)
        own_ref[1, place] = jnp.where(device == owner, fresh, 0.0)

    slots = code_ref.shape[0]
    places = placement[...] - device * slots
    row = lax.broadcasted_iota(jnp.int32, places.shape, 0)
    length = jnp.zeros_like(places)
    place = jnp.zeros_like(places)
    for r in range(lengths.shape[0]):
        length = jnp.where(row == r, lengths[r], length)
        place = jnp.where(row == r, PLACE[r], place)
    start = lax.broadcasted_iota(jnp.int32, places.shape, 1) * BLOCK
    code = (place << LIVE_BITS) + jnp.clip(length - start, 0, BLOCK)
    high = code << CODE_BITS
    for slot in range(0, slots, 2):
        both = jnp.sum(jnp.where(places == slot, code, jnp.where(places == slot + 1, high, 0)))
        code_ref[slot] = both & ((1 << CODE_BITS) - 1)
        code_ref[slot + 1] = both >> CODE_BITS


def hold_kernel(spread_ref, key_cache_hbm, value_cache_hbm, out_ref):
    pass


def attention_kernel(
    code_ref,
    query_ref,
    own_ref,
    key_ref,
    value_ref,
    out_ref,
    scores,
    peaks,
    masses,
    sums,
):
    slots, block, _ = key_ref.shape
    rows = query_ref.shape[0]
    contract_last = (((1,), (1,)), ((), ()))
    position = lax.broadcasted_iota(jnp.int32, (GROUP, block), 1)
    lane = lax.broadcasted_iota(jnp.int32, (rows, GROUP, 128), 2)
    peaks[...] = own_ref[0]
    held = []
    for slot in range(slots):
        code = code_ref[slot]
        held.append((code >> LIVE_BITS, code & ((1 << LIVE_BITS) - 1)))
    for slot, (row, live) in enumerate(held):
        s = lax.dot_general(
            query_ref[row], key_ref[slot], contract_last, preferred_element_type=jnp.float32
        )
        s = jnp.where(position < live, s * SCALE, LOW)
        scores[slot] = s
        top = s[:, :128]
        for part in range(1, block // 128):
            top = jnp.maximum(top, s[:, part * 128 : (part + 1) * 128])
        peaks[row] = jnp.maximum(peaks[row], top)
    top = jnp.max(peaks[...], axis=-1, keepdims=True)
    top = top.astype(jnp.bfloat16).astype(jnp.float32)
    peaks[...] = jnp.broadcast_to(top, peaks.shape)
    own_weight = jnp.exp(own_ref[0] - peaks[...])
    masses[...] = jnp.where(lane == 0, own_weight, 0.0)
    sums[...] = own_weight.astype(jnp.bfloat16).astype(jnp.float32) * own_ref[1]
    for slot, (row, _) in enumerate(held):
        w = jnp.exp(scores[slot] - jnp.tile(peaks[row], (1, block // 128)))
        mass = w[:, :128]
        for part in range(1, block // 128):
            mass = mass + w[:, part * 128 : (part + 1) * 128]
        masses[row] = masses[row] + mass
        sums[row] = sums[row] + jnp.dot(
            w.astype(jnp.bfloat16), value_ref[slot], preferred_element_type=jnp.float32
        )
    mass = jnp.sum(masses[...], axis=-1, keepdims=True)
    high = mass.astype(jnp.bfloat16).astype(jnp.float32)
    low = mass - high
    lane = lane[0]
    share = rows // SETS
    for which in range(SETS):
        extra = jnp.zeros((GROUP, 128), jnp.float32)
        for i in range(share):
            place, at = which * share + i, i * (128 // share)
            extra = jnp.where(lane == at, peaks[place], extra)
            extra = jnp.where(lane == at + 1, high[place], extra)
            extra = jnp.where(lane == at + 2, low[place], extra)
        block = sums[which * share : (which + 1) * share].reshape(share * GROUP, 128)
        block = jnp.concatenate([block, extra], axis=0).astype(jnp.bfloat16)
        for place in range(out_ref.shape[0]):
            if set_of(ORDER[place]) == which:
                out_ref[place] = block


def set_of(device):
    return device // X % 2 * X + device % X


def finish_kernel(parts_ref, out_ref):
    parts = parts_ref[...].astype(jnp.float32)
    share = parts.shape[1] // GROUP - 1
    extra = parts[:, share * GROUP :]
    factor = jnp.exp(extra - jnp.max(extra, axis=0, keepdims=True))
    masses = pltpu.roll(extra, 127, 2) + pltpu.roll(extra, 126, 2)
    factor = factor / jnp.sum(masses * factor, axis=0, keepdims=True)
    attended = []
    for i in range(share):
        at = i * (128 // share)
        partial = parts[:, i * GROUP : (i + 1) * GROUP]
        attended.append(jnp.sum(partial * factor[:, :, at : at + 1], axis=0))
    attended = jnp.concatenate(attended, axis=0).astype(jnp.bfloat16)
    out_ref[...] = jnp.broadcast_to(attended[None], out_ref.shape)


def project_kernel(attended_ref, w_ref, out_ref):
    sets = attended_ref[...].astype(jnp.float32)
    share = sets.shape[1] // GROUP
    rows = []
    for place in PLACE:
        at = place % share * GROUP
        rows.append(sets[place // share ^ FAR_SET, at : at + GROUP])
    heads = jnp.swapaxes(jnp.stack(rows), 0, 1).astype(jnp.bfloat16)
    total = None
    for head in range(GROUP):
        term = jnp.dot(
            heads[head],
            w_ref[head * HEAD_SIZE : (head + 1) * HEAD_SIZE, :],
            preferred_element_type=jnp.float32,
        )
        total = term if total is None else total + term
    ranks, packed, full = out_ref.shape
    width = total.shape[1] // ranks
    for rank in range(ranks):
        block = total[:, rank * width : (rank + 1) * width]
        out_ref[rank ^ FAR_RANK] = jnp.concatenate(
            [block[i * packed : (i + 1) * packed] for i in range(full // width)], axis=1
        )


def sum_kernel(terms_ref, out_ref):
    total = jnp.sum(terms_ref[...], axis=0)
    width = out_ref.shape[1]
    out_ref[...] = jnp.concatenate(
        [total[:, i * width : (i + 1) * width] for i in range(total.shape[1] // width)], axis=0
    ).astype(jnp.bfloat16)


def exchange(x, axis, groups):
    return lax.all_to_all(x, axis, 0, 0, tiled=True, axis_index_groups=groups)


def in_hbm(x):
    return pltpu.with_memory_space_constraint(x, pltpu.HBM)


def call(kernel, name, out_shape, in_specs, scratch_shapes=(), megabytes=2):
    return pl.pallas_call(
        kernel,
        out_shape=out_shape,
        in_specs=in_specs,
        out_specs=jax.tree.map(lambda _: VMEM, out_shape),
        scratch_shapes=scratch_shapes,
        compiler_params=pltpu.CompilerParams(vmem_limit_bytes=megabytes << 20),
        name=name,
    )


def shards(
    queries,
    fresh_keys,
    fresh_values,
    key_cache_blocks,
    value_cache_blocks,
    lengths,
    placement,
    w_out,
):
    rows = lengths.shape[0]
    slots, block, _ = key_cache_blocks.shape
    ranks = lax.axis_size("tensor")
    everyone = [ORDER]
    blocks = [[at + (i ^ FAR_SET) for i in range(SETS)] for at in range(0, rows, SETS)]
    share = rows // SETS * GROUP
    per_row = jax.ShapeDtypeStruct((rows, GROUP, HEAD_SIZE), jnp.bfloat16)

    small = (queries, fresh_keys, fresh_values, lengths, placement)
    room = [pltpu.VMEM(a.shape, a.dtype) for a in small]
    room[3] = pltpu.SMEM(lengths.shape, jnp.int32)
    spread, own, codes = pl.pallas_call(
        spread_kernel,
        out_shape=(
            per_row,
            jax.ShapeDtypeStruct((2, *per_row.shape), jnp.float32),
            pltpu.SMEM((slots,), jnp.int32),
        ),
        in_specs=[ANY] * len(small),
        out_specs=(VMEM, VMEM, SMEM),
        scratch_shapes=room + [pltpu.SemaphoreType.DMA((len(small),))],
        compiler_params=pltpu.CompilerParams(vmem_limit_bytes=2 << 20),
        name="spread",
    )(*map(in_hbm, small))
    spread = pl.pallas_call(
        hold_kernel,
        out_shape=per_row,
        in_specs=[VMEM, ANY, ANY],
        out_specs=VMEM,
        input_output_aliases={0: 0},
        compiler_params=pltpu.CompilerParams(vmem_limit_bytes=2 << 20),
        name="hold",
    )(spread, in_hbm(key_cache_blocks), in_hbm(value_cache_blocks))
    every_query = exchange(spread, "attn", everyone)
    state = pltpu.VMEM((rows, GROUP, 128), jnp.float32)
    partials = call(
        attention_kernel,
        "attention",
        jax.ShapeDtypeStruct((rows, share + GROUP, HEAD_SIZE), jnp.bfloat16),
        [SMEM, VMEM, VMEM, VMEM, VMEM],
        [pltpu.VMEM((slots, GROUP, block), jnp.float32), state, state, state],
        4,
    )(codes, every_query, own, key_cache_blocks, value_cache_blocks)
    partials = exchange(partials, "attn", everyone)
    attended = call(
        finish_kernel,
        "finish",
        jax.ShapeDtypeStruct((SETS, share, HEAD_SIZE), jnp.bfloat16),
        [VMEM],
    )(partials)
    attended = exchange(attended, "attn", blocks)

    width = w_out.shape[1] // ranks
    terms = call(
        project_kernel,
        "project",
        jax.ShapeDtypeStruct((ranks, rows * width // 128, 128), jnp.float32),
        [VMEM, VMEM],
        (),
        4,
    )(attended, w_out)
    terms = exchange(terms, "tensor", [[i ^ FAR_RANK for i in range(ranks)]])
    return call(sum_kernel, "sum", jax.ShapeDtypeStruct((rows, width), jnp.bfloat16), [VMEM])(terms)


def solution(mesh):
    return jax.shard_map(
        shards,
        mesh=mesh,
        in_specs=(
            P("attn", "tensor"),
            P("attn", "tensor"),
            P("attn", "tensor"),
            P("attn", None, "tensor"),
            P("attn", None, "tensor"),
            P(),
            P(),
            P("tensor", "attn"),
        ),
        out_specs=P(None, ("attn", "tensor")),
        check_vma=False,
    )
```

```python
import math

import jax
import jax.numpy as jnp
from jax import lax
from jax.experimental import pallas as pl
from jax.experimental.pallas import tpu as pltpu
from jax.sharding import PartitionSpec as P

QUERY_HEADS = 64
KEY_VALUE_HEADS = 8
HEAD_SIZE = 128
BLOCK = 512
GROUP = QUERY_HEADS // KEY_VALUE_HEADS
SCALE = 1.0 / math.sqrt(HEAD_SIZE)
LOW = -(2.0**99)
FAR_RANK = 4
Z = 8
X = 4


def hops(device):
    return abs(device // X - Z // 2) + abs(device % X - X // 2)


ORDER = sorted(range(Z * X), key=lambda device: (hops(device), device))
PLACE = [ORDER.index(device) for device in range(Z * X)]

SETS = 2 * X
FAR_SET = 6
LIVE_BITS = 10
CODE_BITS = LIVE_BITS + 5

VMEM = pl.BlockSpec(memory_space=pltpu.VMEM)
SMEM = pl.BlockSpec(memory_space=pltpu.SMEM)
ANY = pl.BlockSpec(memory_space=pl.ANY)


def spread_kernel(
    query_hbm,
    key_hbm,
    value_hbm,
    lengths_hbm,
    placement_hbm,
    out_ref,
    own_ref,
    code_ref,
    query,
    key,
    value,
    lengths,
    placement,
    sems,
):
    pairs = (
        (query_hbm, query),
        (key_hbm, key),
        (value_hbm, value),
        (lengths_hbm, lengths),
        (placement_hbm, placement),
    )
    copies = [pltpu.make_async_copy(*pair, sems.at[i]) for i, pair in enumerate(pairs)]
    for copy in copies:
        copy.start()
    for copy in copies[:3]:
        copy.wait()
    wide = query[...].astype(jnp.float32)
    heads = [wide[:, head * HEAD_SIZE : (head + 1) * HEAD_SIZE] for head in range(GROUP)]
    heads = jnp.concatenate(heads, axis=0)
    out_ref[...] = jnp.broadcast_to(heads.astype(jnp.bfloat16)[None], out_ref.shape)
    score = SCALE * jnp.sum(heads * key[...].astype(jnp.float32), axis=-1, keepdims=True)
    device = lax.axis_index("attn")
    score = jnp.broadcast_to(score, (GROUP, HEAD_SIZE))
    fresh = jnp.broadcast_to(value[...].astype(jnp.float32), (GROUP, HEAD_SIZE))
    for place, owner in enumerate(ORDER):
        own_ref[0, place] = jnp.where(device == owner, score, LOW)
        own_ref[1, place] = jnp.where(device == owner, fresh, 0.0)

    for copy in copies[3:]:
        copy.wait()
    slots = code_ref.shape[0]
    places = placement[...] - device * slots
    row = lax.broadcasted_iota(jnp.int32, places.shape, 0)
    length = jnp.zeros_like(places)
    place = jnp.zeros_like(places)
    for r in range(lengths.shape[0]):
        length = jnp.where(row == r, lengths[r], length)
        place = jnp.where(row == r, PLACE[r], place)
    start = lax.broadcasted_iota(jnp.int32, places.shape, 1) * BLOCK
    code = (place << LIVE_BITS) + jnp.clip(length - start, 0, BLOCK)
    high = code << CODE_BITS
    for slot in range(0, slots, 2):
        both = jnp.sum(jnp.where(places == slot, code, jnp.where(places == slot + 1, high, 0)))
        code_ref[slot] = both & ((1 << CODE_BITS) - 1)
        code_ref[slot + 1] = both >> CODE_BITS


def hold_kernel(spread_ref, key_cache_hbm, value_cache_hbm, out_ref):
    pass


def attention_kernel(
    code_ref,
    query_ref,
    own_ref,
    key_ref,
    value_ref,
    out_ref,
    scores,
    peaks,
    masses,
    sums,
):
    slots, block, _ = key_ref.shape
    rows = query_ref.shape[0]
    contract_last = (((1,), (1,)), ((), ()))
    position = lax.broadcasted_iota(jnp.int32, (GROUP, block), 1)
    lane = lax.broadcasted_iota(jnp.int32, (rows, GROUP, 128), 2)
    peaks[...] = own_ref[0]
    held = []
    for slot in range(slots):
        code = code_ref[slot]
        held.append((code >> LIVE_BITS, code & ((1 << LIVE_BITS) - 1)))
    for slot, (row, live) in enumerate(held):
        s = lax.dot_general(
            query_ref[row], key_ref[slot], contract_last, preferred_element_type=jnp.float32
        )
        s = jnp.where(position < live, s * SCALE, LOW)
        scores[slot] = s
        top = s[:, :128]
        for part in range(1, block // 128):
            top = jnp.maximum(top, s[:, part * 128 : (part + 1) * 128])
        peaks[row] = jnp.maximum(peaks[row], top)
    top = jnp.max(peaks[...], axis=-1, keepdims=True)
    top = top.astype(jnp.bfloat16).astype(jnp.float32)
    peaks[...] = jnp.broadcast_to(top, peaks.shape)
    own_weight = jnp.exp(own_ref[0] - peaks[...])
    masses[...] = jnp.where(lane == 0, own_weight, 0.0)
    sums[...] = own_weight.astype(jnp.bfloat16).astype(jnp.float32) * own_ref[1]
    for slot, (row, _) in enumerate(held):
        w = jnp.exp(scores[slot] - jnp.tile(peaks[row], (1, block // 128)))
        mass = w[:, :128]
        for part in range(1, block // 128):
            mass = mass + w[:, part * 128 : (part + 1) * 128]
        masses[row] = masses[row] + mass
        sums[row] = sums[row] + jnp.dot(
            w.astype(jnp.bfloat16), value_ref[slot], preferred_element_type=jnp.float32
        )
    mass = jnp.sum(masses[...], axis=-1, keepdims=True)
    high = mass.astype(jnp.bfloat16).astype(jnp.float32)
    low = mass - high
    lane = lane[0]
    share = rows // SETS
    for which in range(SETS):
        extra = jnp.zeros((GROUP, 128), jnp.float32)
        for i in range(share):
            place, at = which * share + i, i * (128 // share)
            extra = jnp.where(lane == at, peaks[place], extra)
            extra = jnp.where(lane == at + 1, high[place], extra)
            extra = jnp.where(lane == at + 2, low[place], extra)
        block = sums[which * share : (which + 1) * share].reshape(share * GROUP, 128)
        block = jnp.concatenate([block, extra], axis=0).astype(jnp.bfloat16)
        for place in range(out_ref.shape[0]):
            if set_of(ORDER[place]) == which:
                out_ref[place] = block


def set_of(device):
    return device // X % 2 * X + device % X


def finish_kernel(parts_ref, out_ref):
    parts = parts_ref[...].astype(jnp.float32)
    share = parts.shape[1] // GROUP - 1
    extra = parts[:, share * GROUP :]
    factor = jnp.exp(extra - jnp.max(extra, axis=0, keepdims=True))
    masses = pltpu.roll(extra, 127, 2) + pltpu.roll(extra, 126, 2)
    factor = factor / jnp.sum(masses * factor, axis=0, keepdims=True)
    attended = []
    for i in range(share):
        at = i * (128 // share)
        partial = parts[:, i * GROUP : (i + 1) * GROUP]
        attended.append(jnp.sum(partial * factor[:, :, at : at + 1], axis=0))
    attended = jnp.concatenate(attended, axis=0).astype(jnp.bfloat16)
    out_ref[...] = jnp.broadcast_to(attended[None], out_ref.shape)


def project_kernel(attended_ref, w_ref, out_ref):
    sets = attended_ref[...].astype(jnp.float32)
    share = sets.shape[1] // GROUP
    rows = []
    for place in PLACE:
        at = place % share * GROUP
        rows.append(sets[place // share ^ FAR_SET, at : at + GROUP])
    heads = jnp.swapaxes(jnp.stack(rows), 0, 1).astype(jnp.bfloat16)
    total = None
    for head in range(GROUP):
        term = jnp.dot(
            heads[head],
            w_ref[head * HEAD_SIZE : (head + 1) * HEAD_SIZE, :],
            preferred_element_type=jnp.float32,
        )
        total = term if total is None else total + term
    ranks, packed, full = out_ref.shape
    width = total.shape[1] // ranks
    for rank in range(ranks):
        block = total[:, rank * width : (rank + 1) * width]
        out_ref[rank ^ FAR_RANK] = jnp.concatenate(
            [block[i * packed : (i + 1) * packed] for i in range(full // width)], axis=1
        ).astype(out_ref.dtype)


def sum_kernel(terms_ref, out_ref):
    total = jnp.sum(terms_ref[...].astype(jnp.float32), axis=0)
    width = out_ref.shape[1]
    out_ref[...] = jnp.concatenate(
        [total[:, i * width : (i + 1) * width] for i in range(total.shape[1] // width)], axis=0
    ).astype(jnp.bfloat16)


def exchange(x, axis, groups):
    return lax.all_to_all(x, axis, 0, 0, tiled=True, axis_index_groups=groups)


def in_hbm(x):
    return pltpu.with_memory_space_constraint(x, pltpu.HBM)


def call(kernel, name, out_shape, in_specs, scratch_shapes=(), megabytes=2):
    return pl.pallas_call(
        kernel,
        out_shape=out_shape,
        in_specs=in_specs,
        out_specs=jax.tree.map(lambda _: VMEM, out_shape),
        scratch_shapes=scratch_shapes,
        compiler_params=pltpu.CompilerParams(vmem_limit_bytes=megabytes << 20),
        name=name,
    )


def shards(
    queries,
    fresh_keys,
    fresh_values,
    key_cache_blocks,
    value_cache_blocks,
    lengths,
    placement,
    w_out,
):
    rows = lengths.shape[0]
    slots, block, _ = key_cache_blocks.shape
    ranks = lax.axis_size("tensor")
    everyone = [ORDER]
    blocks = [[at + (i ^ FAR_SET) for i in range(SETS)] for at in range(0, rows, SETS)]
    share = rows // SETS * GROUP
    per_row = jax.ShapeDtypeStruct((rows, GROUP, HEAD_SIZE), jnp.bfloat16)

    small = (queries, fresh_keys, fresh_values, lengths, placement)
    room = [pltpu.VMEM(a.shape, a.dtype) for a in small]
    room[3] = pltpu.SMEM(lengths.shape, jnp.int32)
    spread, own, codes = pl.pallas_call(
        spread_kernel,
        out_shape=(
            per_row,
            jax.ShapeDtypeStruct((2, *per_row.shape), jnp.float32),
            pltpu.SMEM((slots,), jnp.int32),
        ),
        in_specs=[ANY] * len(small),
        out_specs=(VMEM, VMEM, SMEM),
        scratch_shapes=room + [pltpu.SemaphoreType.DMA((len(small),))],
        compiler_params=pltpu.CompilerParams(vmem_limit_bytes=2 << 20),
        name="spread",
    )(*map(in_hbm, small))
    spread = pl.pallas_call(
        hold_kernel,
        out_shape=per_row,
        in_specs=[VMEM, ANY, ANY],
        out_specs=VMEM,
        input_output_aliases={0: 0},
        compiler_params=pltpu.CompilerParams(vmem_limit_bytes=2 << 20),
        name="hold",
    )(spread, in_hbm(key_cache_blocks), in_hbm(value_cache_blocks))
    every_query = exchange(spread, "attn", everyone)
    state = pltpu.VMEM((rows, GROUP, 128), jnp.float32)
    partials = call(
        attention_kernel,
        "attention",
        jax.ShapeDtypeStruct((rows, share + GROUP, HEAD_SIZE), jnp.bfloat16),
        [SMEM, VMEM, VMEM, VMEM, VMEM],
        [pltpu.VMEM((slots, GROUP, block), jnp.float32), state, state, state],
        4,
    )(codes, every_query, own, key_cache_blocks, value_cache_blocks)
    partials = exchange(partials, "attn", everyone)
    attended = call(
        finish_kernel,
        "finish",
        jax.ShapeDtypeStruct((SETS, share, HEAD_SIZE), jnp.bfloat16),
        [VMEM],
    )(partials)
    attended = exchange(attended, "attn", blocks)

    width = w_out.shape[1] // ranks
    terms = call(
        project_kernel,
        "project",
        jax.ShapeDtypeStruct((ranks, rows * width // 128, 128), jnp.bfloat16),
        [VMEM, VMEM],
        (),
        4,
    )(attended, w_out)
    terms = exchange(terms, "tensor", [[i ^ FAR_RANK for i in range(ranks)]])
    return call(sum_kernel, "sum", jax.ShapeDtypeStruct((rows, width), jnp.bfloat16), [VMEM])(terms)


def solution(mesh):
    return jax.shard_map(
        shards,
        mesh=mesh,
        in_specs=(
            P("attn", "tensor"),
            P("attn", "tensor"),
            P("attn", "tensor"),
            P("attn", None, "tensor"),
            P("attn", None, "tensor"),
            P(),
            P(),
            P("tensor", "attn"),
        ),
        out_specs=P(None, ("attn", "tensor")),
        check_vma=False,
    )
```

```python
import math

import jax
import jax.numpy as jnp
from jax import lax
from jax.experimental import pallas as pl
from jax.experimental.pallas import tpu as pltpu
from jax.sharding import PartitionSpec as P

QUERY_HEADS = 64
KEY_VALUE_HEADS = 8
HEAD_SIZE = 128
BLOCK = 512
GROUP = QUERY_HEADS // KEY_VALUE_HEADS
SCALE = 1.0 / math.sqrt(HEAD_SIZE)
LOW = -(2.0**99)
FAR_RANK = 4
Z = 8
FAR_Z = 5
X = 4


def hops(device):
    along_z = (device // X - FAR_Z) % Z
    return min(along_z, Z - along_z) + abs(device % X - X // 2)


ORDER = sorted(range(Z * X), key=lambda device: (hops(device), device))
PLACE = [ORDER.index(device) for device in range(Z * X)]

SETS = 2 * X
FAR_SET = 6
LIVE_BITS = 10
CODE_BITS = LIVE_BITS + 5

VMEM = pl.BlockSpec(memory_space=pltpu.VMEM)
SMEM = pl.BlockSpec(memory_space=pltpu.SMEM)
ANY = pl.BlockSpec(memory_space=pl.ANY)


def spread_kernel(
    query_hbm,
    key_hbm,
    value_hbm,
    lengths_hbm,
    placement_hbm,
    out_ref,
    own_ref,
    code_ref,
    query,
    key,
    value,
    lengths,
    placement,
    sems,
):
    pairs = (
        (query_hbm, query),
        (key_hbm, key),
        (value_hbm, value),
        (lengths_hbm, lengths),
        (placement_hbm, placement),
    )
    copies = [pltpu.make_async_copy(*pair, sems.at[i]) for i, pair in enumerate(pairs)]
    for copy in copies:
        copy.start()
    for copy in copies:
        copy.wait()
    wide = query[...].astype(jnp.float32)
    heads = [wide[:, head * HEAD_SIZE : (head + 1) * HEAD_SIZE] for head in range(GROUP)]
    heads = jnp.concatenate(heads, axis=0)
    out_ref[...] = jnp.broadcast_to(heads.astype(jnp.bfloat16)[None], out_ref.shape)
    score = SCALE * jnp.sum(heads * key[...].astype(jnp.float32), axis=-1, keepdims=True)
    device = lax.axis_index("attn")
    score = jnp.broadcast_to(score, (GROUP, HEAD_SIZE))
    fresh = jnp.broadcast_to(value[...].astype(jnp.float32), (GROUP, HEAD_SIZE))
    for place, owner in enumerate(ORDER):
        own_ref[0, place] = jnp.where(device == owner, score, LOW)
        own_ref[1, place] = jnp.where(device == owner, fresh, 0.0)

    slots = code_ref.shape[0]
    places = placement[...] - device * slots
    row = lax.broadcasted_iota(jnp.int32, places.shape, 0)
    length = jnp.zeros_like(places)
    place = jnp.zeros_like(places)
    for r in range(lengths.shape[0]):
        length = jnp.where(row == r, lengths[r], length)
        place = jnp.where(row == r, PLACE[r], place)
    start = lax.broadcasted_iota(jnp.int32, places.shape, 1) * BLOCK
    code = (place << LIVE_BITS) + jnp.clip(length - start, 0, BLOCK)
    high = code << CODE_BITS
    for slot in range(0, slots, 2):
        both = jnp.sum(jnp.where(places == slot, code, jnp.where(places == slot + 1, high, 0)))
        code_ref[slot] = both & ((1 << CODE_BITS) - 1)
        code_ref[slot + 1] = both >> CODE_BITS


def hold_kernel(spread_ref, key_cache_hbm, value_cache_hbm, out_ref):
    pass


def attention_kernel(
    code_ref,
    query_ref,
    own_ref,
    key_ref,
    value_ref,
    out_ref,
    scores,
    peaks,
    masses,
    sums,
):
    slots, block, _ = key_ref.shape
    rows = query_ref.shape[0]
    contract_last = (((1,), (1,)), ((), ()))
    position = lax.broadcasted_iota(jnp.int32, (GROUP, block), 1)
    lane = lax.broadcasted_iota(jnp.int32, (rows, GROUP, 128), 2)
    peaks[...] = own_ref[0]
    held = []
    for slot in range(slots):
        code = code_ref[slot]
        held.append((code >> LIVE_BITS, code & ((1 << LIVE_BITS) - 1)))
    for slot, (row, live) in enumerate(held):
        s = lax.dot_general(
            query_ref[row], key_ref[slot], contract_last, preferred_element_type=jnp.float32
        )
        s = jnp.where(position < live, s * SCALE, LOW)
        scores[slot] = s
        top = s[:, :128]
        for part in range(1, block // 128):
            top = jnp.maximum(top, s[:, part * 128 : (part + 1) * 128])
        peaks[row] = jnp.maximum(peaks[row], top)
    top = jnp.max(peaks[...], axis=-1, keepdims=True)
    top = top.astype(jnp.bfloat16).astype(jnp.float32)
    peaks[...] = jnp.broadcast_to(top, peaks.shape)
    own_weight = jnp.exp(own_ref[0] - peaks[...])
    masses[...] = jnp.where(lane == 0, own_weight, 0.0)
    sums[...] = own_weight.astype(jnp.bfloat16).astype(jnp.float32) * own_ref[1]
    for slot, (row, _) in enumerate(held):
        w = jnp.exp(scores[slot] - jnp.tile(peaks[row], (1, block // 128)))
        mass = w[:, :128]
        for part in range(1, block // 128):
            mass = mass + w[:, part * 128 : (part + 1) * 128]
        masses[row] = masses[row] + mass
        sums[row] = sums[row] + jnp.dot(
            w.astype(jnp.bfloat16), value_ref[slot], preferred_element_type=jnp.float32
        )
    mass = jnp.sum(masses[...], axis=-1, keepdims=True)
    high = mass.astype(jnp.bfloat16).astype(jnp.float32)
    low = mass - high
    lane = lane[0]
    share = rows // SETS
    for which in range(SETS):
        extra = jnp.zeros((GROUP, 128), jnp.float32)
        for i in range(share):
            place, at = which * share + i, i * (128 // share)
            extra = jnp.where(lane == at, peaks[place], extra)
            extra = jnp.where(lane == at + 1, high[place], extra)
            extra = jnp.where(lane == at + 2, low[place], extra)
        block = sums[which * share : (which + 1) * share].reshape(share * GROUP, 128)
        block = jnp.concatenate([block, extra], axis=0).astype(jnp.bfloat16)
        for place in range(out_ref.shape[0]):
            if set_of(ORDER[place]) == which:
                out_ref[place] = block


def set_of(device):
    return device // X % 2 * X + device % X


def finish_kernel(parts_ref, out_ref):
    parts = parts_ref[...].astype(jnp.float32)
    share = parts.shape[1] // GROUP - 1
    extra = parts[:, share * GROUP :]
    factor = jnp.exp(extra - jnp.max(extra, axis=0, keepdims=True))
    masses = pltpu.roll(extra, 127, 2) + pltpu.roll(extra, 126, 2)
    factor = factor / jnp.sum(masses * factor, axis=0, keepdims=True)
    attended = []
    for i in range(share):
        at = i * (128 // share)
        partial = parts[:, i * GROUP : (i + 1) * GROUP]
        attended.append(jnp.sum(partial * factor[:, :, at : at + 1], axis=0))
    attended = jnp.concatenate(attended, axis=0).astype(jnp.bfloat16)
    out_ref[...] = jnp.broadcast_to(attended[None], out_ref.shape)


def project_kernel(attended_ref, w_ref, out_ref):
    sets = attended_ref[...].astype(jnp.float32)
    share = sets.shape[1] // GROUP
    rows = []
    for place in PLACE:
        at = place % share * GROUP
        rows.append(sets[place // share ^ FAR_SET, at : at + GROUP])
    heads = jnp.swapaxes(jnp.stack(rows), 0, 1).astype(jnp.bfloat16)
    total = None
    for head in range(GROUP):
        term = jnp.dot(
            heads[head],
            w_ref[head * HEAD_SIZE : (head + 1) * HEAD_SIZE, :],
            preferred_element_type=jnp.float32,
        )
        total = term if total is None else total + term
    ranks, packed, full = out_ref.shape
    width = total.shape[1] // ranks
    for rank in range(ranks):
        block = total[:, rank * width : (rank + 1) * width]
        out_ref[rank ^ FAR_RANK] = jnp.concatenate(
            [block[i * packed : (i + 1) * packed] for i in range(full // width)], axis=1
        )


def sum_kernel(terms_ref, out_ref):
    total = jnp.sum(terms_ref[...], axis=0)
    width = out_ref.shape[1]
    out_ref[...] = jnp.concatenate(
        [total[:, i * width : (i + 1) * width] for i in range(total.shape[1] // width)], axis=0
    ).astype(jnp.bfloat16)


def exchange(x, axis, groups):
    return lax.all_to_all(x, axis, 0, 0, tiled=True, axis_index_groups=groups)


def in_hbm(x):
    return pltpu.with_memory_space_constraint(x, pltpu.HBM)


def call(kernel, name, out_shape, in_specs, scratch_shapes=(), megabytes=2):
    return pl.pallas_call(
        kernel,
        out_shape=out_shape,
        in_specs=in_specs,
        out_specs=jax.tree.map(lambda _: VMEM, out_shape),
        scratch_shapes=scratch_shapes,
        compiler_params=pltpu.CompilerParams(vmem_limit_bytes=megabytes << 20),
        name=name,
    )


def shards(
    queries,
    fresh_keys,
    fresh_values,
    key_cache_blocks,
    value_cache_blocks,
    lengths,
    placement,
    w_out,
):
    rows = lengths.shape[0]
    slots, block, _ = key_cache_blocks.shape
    ranks = lax.axis_size("tensor")
    everyone = [ORDER]
    blocks = [[at + (i ^ FAR_SET) for i in range(SETS)] for at in range(0, rows, SETS)]
    share = rows // SETS * GROUP
    per_row = jax.ShapeDtypeStruct((rows, GROUP, HEAD_SIZE), jnp.bfloat16)

    small = (queries, fresh_keys, fresh_values, lengths, placement)
    room = [pltpu.VMEM(a.shape, a.dtype) for a in small]
    room[3] = pltpu.SMEM(lengths.shape, jnp.int32)
    spread, own, codes = pl.pallas_call(
        spread_kernel,
        out_shape=(
            per_row,
            jax.ShapeDtypeStruct((2, *per_row.shape), jnp.float32),
            pltpu.SMEM((slots,), jnp.int32),
        ),
        in_specs=[ANY] * len(small),
        out_specs=(VMEM, VMEM, SMEM),
        scratch_shapes=room + [pltpu.SemaphoreType.DMA((len(small),))],
        compiler_params=pltpu.CompilerParams(vmem_limit_bytes=2 << 20),
        name="spread",
    )(*map(in_hbm, small))
    spread = pl.pallas_call(
        hold_kernel,
        out_shape=per_row,
        in_specs=[VMEM, ANY, ANY],
        out_specs=VMEM,
        input_output_aliases={0: 0},
        compiler_params=pltpu.CompilerParams(vmem_limit_bytes=2 << 20),
        name="hold",
    )(spread, in_hbm(key_cache_blocks), in_hbm(value_cache_blocks))
    every_query = exchange(spread, "attn", everyone)
    state = pltpu.VMEM((rows, GROUP, 128), jnp.float32)
    partials = call(
        attention_kernel,
        "attention",
        jax.ShapeDtypeStruct((rows, share + GROUP, HEAD_SIZE), jnp.bfloat16),
        [SMEM, VMEM, VMEM, VMEM, VMEM],
        [pltpu.VMEM((slots, GROUP, block), jnp.float32), state, state, state],
        4,
    )(codes, every_query, own, key_cache_blocks, value_cache_blocks)
    partials = exchange(partials, "attn", everyone)
    attended = call(
        finish_kernel,
        "finish",
        jax.ShapeDtypeStruct((SETS, share, HEAD_SIZE), jnp.bfloat16),
        [VMEM],
    )(partials)
    attended = exchange(attended, "attn", blocks)

    width = w_out.shape[1] // ranks
    terms = call(
        project_kernel,
        "project",
        jax.ShapeDtypeStruct((ranks, rows * width // 128, 128), jnp.float32),
        [VMEM, VMEM],
        (),
        4,
    )(attended, w_out)
    terms = exchange(terms, "tensor", [[i ^ FAR_RANK for i in range(ranks)]])
    return call(sum_kernel, "sum", jax.ShapeDtypeStruct((rows, width), jnp.bfloat16), [VMEM])(terms)


def solution(mesh):
    return jax.shard_map(
        shards,
        mesh=mesh,
        in_specs=(
            P("attn", "tensor"),
            P("attn", "tensor"),
            P("attn", "tensor"),
            P("attn", None, "tensor"),
            P("attn", None, "tensor"),
            P(),
            P(),
            P("tensor", "attn"),
        ),
        out_specs=P(None, ("attn", "tensor")),
        check_vma=False,
    )
```
